32 devices in a mesh: sec: 2 (over y), gx: 4 (over z), gy: 4 (over x, core).
Axes of the slice: x: 2, y: 2, z: 4, core: 2. Of those that a mesh axis runs over, the one named last changes fastest.
Arguments:
- model_state: float32 [2, 3, 32, 64, 2048], P('sec', None, None, 'gx', 'gy'), may hold values from -6 to 6
- wave_speed: float32 [2, 64, 2048], P('sec', 'gx', 'gy'), may hold values from 0.05 to 0.45
- wet_mask: int32 [2, 64, 2048], P('sec', 'gx', 'gy'), may hold values 0 or 1
- vertical: float32 [2, 32, 32], P('sec'), may hold values from -1 to 1
- surface_temp: float32 [2, 64, 2048], P('sec', 'gx', 'gy'), may hold values from -6 to 6
- flux_coef: float32 [8, 4], replicated, may hold values from -3 to 3
- heat_gain: float32 [8], replicated, may hold values from -2.5 to 2.5
- pair_tile: int32 [4, 4, 64, 1], P('gx', 'gy'), may hold values from 0 to 3; in each aligned block of 64 rows (0 to 63, 64 to 127, ..., all dimensions but the last counted through in order) at most 32 rows name the same one
- pair_source: int32 [4, 4, 64], P('gx', 'gy'), may hold values from 0 to 31
- pair_target: int32 [4, 4, 64], P('gx', 'gy'), may hold values from 0 to 63
- intersection_weights: bfloat16 [4, 4, 64, 256, 128], P('gx', 'gy'), may hold values from -0.375 to 0.375
Outputs:
- final_state: float32 [2, 3, 32, 64, 2048], P('sec', None, None, 'gx', 'gy')
- surface_temps: float32 [2, 64, 2048], P('sec', 'gx', 'gy')
The draws below stay inside these ranges and needn't reach their ends.
Inputs may be any that keep to these rules, and one draw needn't show every extreme that they name: `pair_tile`: the destination lies in the source tile's column along gy; at most 32 pairs of one atmosphere tile name one ocean tile, and in some tile exactly 32 do.
All inputs are finite; a program needn't handle non-finite values. No bound on the sum of `wet_mask` on one device may be relied on, other than what follows from the above.
Results may differ from the reference program's by a relative error of at most 0.0033.
Values may be sent and summed in bfloat16 or wider, within the bound.
A program may use at most 64 MiB of HBM per device.

```python
import math
import jax
import jax.numpy as jnp
import numpy as np
from jax import lax

LEV = 32
SUBSTEPS = 2
AX = 16
AY = 512
F = 8
RI = 256
RO = 128
KBA = 32
KBO = 64
P_SIZE = 64
CAP = 32
NX = 64
NY = 2048
N_GX = 4
N_GY = 4


def plant(drawn, key, least, high):
    longest = drawn.shape.index(max(drawn.shape))
    spots = []
    for shift in (0, 1):
        where = [jax.random.randint(jax.random.fold_in(key, axis), (), 0, length) for axis, length in enumerate(drawn.shape)]
        where[longest] = (where[longest] + shift) % drawn.shape[longest]
        spots.append(tuple(where))
    return drawn.at[spots[0]].set(least).at[spots[1]].set(high)


def steps_of(own_key, dims, shards, low, largest):
    gain, own = 1.0, jax.random.fold_in(own_key, 6)
    for axis_at, blocks in shards:
        heights = jnp.exp(jax.random.uniform(jax.random.fold_in(own, axis_at), (blocks,), jnp.float32, low / len(shards), largest / len(shards)))
        gain = gain * jnp.repeat(heights, dims[axis_at] // blocks).reshape([-1 if axis == axis_at else 1 for axis in range(len(dims))])
    return gain


def assign_block(stream_key, own, number, rows, amount, top, reach, skew):
    order = jax.random.permutation(stream_key, amount)
    heavy_load, common = portions_of(amount, rows * top, reach, skew, True), portions_of(amount, rows * top, reach, skew, False)
    places = jnp.arange(amount)

    def named(lengths, turn):
        used = int((lengths > 0).sum())
        fixed = max(1, used // 4)
        shifted = fixed + (places - fixed + turn * (used - fixed)) % max(1, amount - fixed)
        return jnp.zeros((amount,), jnp.int32).at[order[jnp.where(places < fixed, places, shifted)]].set(jnp.asarray(lengths, jnp.int32))

    lengths = jnp.where(number % 4 == 0, named(heavy_load, number // 4), named(common, number - number // 4 - 1))
    mixed = jax.random.permutation(jax.random.fold_in(own, 3), amount)
    donor, taker = mixed[0:amount // 2 * 2:2], mixed[1:amount // 2 * 2:2]
    room = jnp.minimum(lengths[donor] - 1, reach - lengths[taker]) // 2
    room = jnp.where((donor == order[0]) | (taker == order[0]) | (lengths[taker] == 0), 0, jnp.maximum(room, 0))
    shifted = jax.random.randint(jax.random.fold_in(own, 4), (amount // 2,), 0, 1 << 20) % (room + 1)
    lengths = lengths.at[donor].add(-shifted).at[taker].add(shifted)
    items = jnp.searchsorted(jnp.cumsum(lengths), jnp.arange(rows * top), side="right").astype(jnp.int32)
    listing = items.reshape(top, rows).T
    listing = listing[jax.random.permutation(jax.random.fold_in(own, 1), rows)]
    turn = jax.random.randint(jax.random.fold_in(own, 2), (rows, 1), 0, top)
    return jnp.take_along_axis(listing, (jnp.arange(top)[None, :] + turn) % top, axis=1)


def portions_of(number_of, total, reach, slope, full):
    loads = [(1 << 20) // math.isqrt(grade ** slope) + 1 for grade in range(1, number_of + 1)]
    largest = reach if full else min(reach, max(-(-total // number_of), total * loads[0] // sum(loads)))
    least = 1 if total - largest >= number_of - 1 else 0
    holding, spare = [largest] + [least] * (number_of - 1), total - largest - least * (number_of - 1)
    while spare > 0:
        candidates = [i for i in range(1, number_of) if holding[i] < largest] or [i for i in range(1, number_of) if holding[i] < reach]
        pool, left = sum([loads[i] for i in candidates]), spare
        for i in candidates:
            extra = min(reach - holding[i], max(1, left * loads[i] // pool), spare)
            holding[i] = holding[i] + extra
            spare = spare - extra
    return np.array(holding)


def noise(key, dims, width, bound, cuts=(), kind=jnp.bfloat16):
    result = width * jax.random.normal(key, dims, jnp.float32)
    if cuts:
        result = result * steps_of(key, dims, cuts, -0.22, 0.18)
    return jnp.clip(result, -bound, bound).astype(kind)


def setup_inputs(seed: int = 0) -> dict:
    key_of = jax.random.split(jax.random.key(seed), 12)
    model_state = noise(key_of[0], (2, 3, LEV, NX, NY), 1.0, 6.0, ((0, 2), (3, 4), (4, 4)), jnp.float32)
    wave_speed = jnp.clip(0.05 + 0.39999999 * jax.random.uniform(key_of[1], (2, NX, NY), jnp.float32) ** steps_of(key_of[1], (2, NX, NY), ((0, 2), (1, 4), (2, 4)), -0.2, 0.2), 0.05, 0.45)
    wet_mask = plant((jax.random.randint(key_of[2], (2, NX, NY), 0, 8) < 7).astype(jnp.int32), jax.random.fold_in(key_of[2], 1), 0, 1)
    vertical = noise(key_of[3], (2, LEV, LEV), LEV ** -0.5, 1.0, ((0, 2),), jnp.float32)
    surface_temp = noise(key_of[4], (2, NX, NY), 1.0, 6.0, ((0, 2), (1, 4), (2, 4)), jnp.float32)
    flux_coef = noise(key_of[5], (F, 4), 0.6, 3.0, (), jnp.float32)
    heat_gain = noise(key_of[6], (F,), 0.5, 2.5, (), jnp.float32)
    pair_tile_keys = jax.random.split(jax.random.fold_in(key_of[7], 1), N_GX * N_GY * P_SIZE // P_SIZE)
    pair_tile_turns = jax.random.permutation(jax.random.fold_in(key_of[7], 3), N_GX * N_GY * P_SIZE // P_SIZE)
    pair_tile = jax.vmap(lambda own, number: assign_block(jax.random.fold_in(key_of[7], 2), own, number, P_SIZE, N_GX, 1, CAP, 1))(pair_tile_keys, pair_tile_turns).reshape((N_GX, N_GY, P_SIZE, 1))
    pair_source = plant(jax.random.randint(key_of[8], (N_GX, N_GY, P_SIZE), 0, KBA), jax.random.fold_in(key_of[8], 1), 0, KBA - 1).astype(jnp.int32)
    pair_target = plant(jax.random.randint(key_of[9], (N_GX, N_GY, P_SIZE), 0, KBO), jax.random.fold_in(key_of[9], 1), 0, KBO - 1).astype(jnp.int32)
    intersection_weights = noise(key_of[10], (N_GX, N_GY, P_SIZE, RI, RO), RI ** -0.5, 0.375, ((0, 4), (1, 4)))
    return {"model_state": model_state, "wave_speed": wave_speed, "wet_mask": wet_mask, "vertical": vertical, "surface_temp": surface_temp, "flux_coef": flux_coef, "heat_gain": heat_gain, "pair_tile": pair_tile, "pair_source": pair_source, "pair_target": pair_target, "intersection_weights": intersection_weights}


HIGHEST_PRECISION = lax.Precision.HIGHEST


def eastern(values):
    return jnp.pad(values, ((0, 0), (0, 1), (0, 0)))[:, 1:, :]


def western(values):
    return jnp.pad(values, ((0, 0), (1, 0), (0, 0)))[:, :-1, :]


def northern(values):
    return jnp.pad(values, ((0, 0), (0, 0), (0, 1)))[:, :, 1:]


def southern(values):
    return jnp.pad(values, ((0, 0), (0, 0), (1, 0)))[:, :, :-1]


def vertical_mix(matrix, right_side):
    return right_side + jnp.einsum("lm,mxy->lxy", matrix, right_side, precision=HIGHEST_PRECISION)


def make_tiles(values):
    return values.reshape(N_GX, AX, N_GY, AY).transpose(0, 2, 1, 3).reshape(N_GX, N_GY, AX * AY)


def join_tiles(values):
    return values.reshape(N_GX, N_GY, AX, AY).transpose(0, 2, 1, 3).reshape(N_GX * AX, N_GY * AY)


def reference(model_state, wave_speed, wet_mask, vertical, surface_temp, flux_coef, heat_gain, pair_tile, pair_source, pair_target, intersection_weights):
    finals = []
    for section in range(2):
        pressure = model_state[section, 0]
        eastward = model_state[section, 1]
        northward = model_state[section, 2]
        sound_speed = wave_speed[section]
        wetness = wet_mask[section].astype(jnp.float32)
        matrix = vertical[section]
        for substep in range(SUBSTEPS):
            divergence = (eastern(eastward) - western(eastward)) + (northern(northward) - southern(northward))
            pressure = vertical_mix(matrix, pressure - sound_speed * divergence)
            eastward = wetness * (eastward - 0.5 * (eastern(pressure) - western(pressure)))
            northward = wetness * (northward - 0.5 * (northern(pressure) - southern(pressure)))
        finals.append(jnp.stack([pressure, eastward, northward]))
    final_state = jnp.stack(finals)

    drivers = jnp.stack([make_tiles(model_state[0, 0, 0]), make_tiles(model_state[0, 1, 0]), make_tiles(model_state[0, 2, 0]), make_tiles(surface_temp[0])], axis=2)
    fluxes = jnp.tanh(jnp.einsum("fk,abkc->abfc", flux_coef, drivers, precision=HIGHEST_PRECISION)).astype(jnp.bfloat16)
    blocks = fluxes.reshape(N_GX, N_GY, F, KBA, RI).transpose(0, 1, 3, 2, 4)
    across = jnp.arange(N_GX, dtype=jnp.int32)[:, None, None]
    within = jnp.arange(N_GY, dtype=jnp.int32)[None, :, None]
    picked = blocks[across, within, pair_source]
    weights_wide = intersection_weights.astype(jnp.float32)
    regridded = jnp.einsum("abpfi,abpio->abpfo", picked.astype(jnp.float32), weights_wide, precision=HIGHEST_PRECISION).astype(jnp.bfloat16)
    target_tile = pair_tile[..., 0]
    ocean_blocks = jnp.zeros((N_GX, N_GY, KBO, F, RO), jnp.float32).at[target_tile, within, pair_target].add(regridded.astype(jnp.float32))
    ocean_flux = ocean_blocks.transpose(0, 1, 3, 2, 4).reshape(N_GX, N_GY, F, KBO * RO)
    heating = jnp.einsum("f,abfc->abc", heat_gain, ocean_flux, precision=HIGHEST_PRECISION)
    ocean_temp = make_tiles(surface_temp[1]) + make_tiles(wet_mask[1].astype(jnp.float32)) * heating
    returned = ocean_temp.astype(jnp.bfloat16).reshape(N_GX, N_GY, KBO, RO)[target_tile, within, pair_target]
    pieces = jnp.einsum("abpio,abpo->abpi", weights_wide, returned.astype(jnp.float32), precision=HIGHEST_PRECISION)
    atmos_blocks = jnp.zeros((N_GX, N_GY, KBA, RI), jnp.float32).at[across, within, pair_source].add(pieces)
    surface_temps = jnp.stack([join_tiles(atmos_blocks.reshape(N_GX, N_GY, AX * AY)), join_tiles(ocean_temp)])
    return final_state, surface_temps
```

```python
import functools

import jax
import jax.numpy as jnp
from jax import lax
from jax.experimental import pallas as pl
from jax.experimental.pallas import tpu as pltpu
from jax.sharding import PartitionSpec as P

MESH = pl.DeviceIdType.MESH
F32 = jnp.float32
BF16 = jnp.bfloat16
LANES = 128
CHUNKS = 8


def iota(shape, axis):
    return lax.broadcasted_iota(jnp.int32, shape, axis)


def split(value, parts):
    pieces = []
    for _ in range(parts):
        piece = value.astype(BF16)
        pieces.append(piece)
        value = value - piece.astype(F32)
    return pieces


def dot(a, b):
    return jnp.dot(a, b, preferred_element_type=F32)


def block_key(index, rows, per_row):
    return (index & (rows - 1)) * per_row + (index >> (rows.bit_length() - 1))


def kernel(
    n_gx,
    n_gy,
    state,
    speed,
    mask,
    vertical,
    temp,
    coef,
    gain,
    tile_in,
    source_in,
    target_in,
    source_s,
    weights,
    final,
    surface,
    raw,
    out,
    wbuf,
    u0,
    p1,
    u1,
    v1,
    p2,
    colsend,
    colrecv,
    ybuf,
    yrecv,
    trecv,
    xbuf,
    load_sem,
    w_sem,
    row_send,
    row_recv,
    col_send,
    col_recv,
    y_send,
    y_recv,
    t_send,
    t_recv,
    x_send,
    x_recv,
    out_sem,
):
    sec = lax.axis_index("sec")
    a = lax.axis_index("gx")
    b = lax.axis_index("gy")
    levels, rows, width = state.shape[2:]
    tiles = width // LANES
    pairs, in_width, out_width = wbuf.shape
    in_per_row = width // in_width
    out_per_row = width // out_width
    in_blocks = rows * in_per_row
    out_blocks = rows * out_per_row
    per_chunk = pairs // CHUNKS

    def load(f, i):
        part = state.at[0, f, :, :, pl.ds(i * LANES, LANES)]
        return pltpu.make_async_copy(part, raw.at[f, i], load_sem.at[f, i])

    def load_weights(i):
        part = pl.ds(i * per_chunk, per_chunk)
        return pltpu.make_async_copy(weights.at[0, 0, part], wbuf.at[part], w_sem.at[i])

    for f in (1, 2, 0):
        for i in range(tiles):
            load(f, i).start()
    for i in range(CHUNKS):
        load_weights(i).start()

    barrier = pltpu.get_barrier_semaphore()
    for s in range(2):
        for t in range(n_gx):

            @pl.when(jnp.logical_or(s != sec, t != a))
            def _():
                pl.semaphore_signal(barrier, inc=1, device_id=(s, t, b), device_id_type=MESH)

    @pl.when(b > 0)
    def _():
        pl.semaphore_signal(barrier, inc=1, device_id=(sec, a, b - 1), device_id_type=MESH)

    @pl.when(b < n_gy - 1)
    def _():
        pl.semaphore_signal(barrier, inc=1, device_id=(sec, a, b + 1), device_id_type=MESH)

    beside = (b > 0).astype(jnp.int32) + (b < n_gy - 1).astype(jnp.int32)

    @pl.when(a == 0)
    def _():
        for buf in (u0, p1, u1, p2):
            buf[0] = jnp.zeros((levels, width), F32)

    @pl.when(a == n_gx - 1)
    def _():
        for buf in (u0, p1, u1, p2):
            buf[rows + 1] = jnp.zeros((levels, width), F32)

    @pl.when(b == 0)
    def _():
        for stage in range(4):
            colrecv[stage, 0] = jnp.zeros((levels, LANES), F32)

    @pl.when(b == n_gy - 1)
    def _():
        for stage in range(4):
            colrecv[stage, 1] = jnp.zeros((levels, LANES), F32)

    def row_copy(stage, buf, side):
        src, dst = (1, rows + 1) if side == 0 else (rows, 0)
        return pltpu.make_async_remote_copy(
            src_ref=buf.at[src],
            dst_ref=buf.at[dst],
            send_sem=row_send.at[stage, side],
            recv_sem=row_recv.at[stage, side],
            device_id=(sec, a - 1 if side == 0 else a + 1, b),
            device_id_type=MESH,
        )

    def col_copy(stage, side):
        return pltpu.make_async_remote_copy(
            src_ref=colsend.at[stage, side],
            dst_ref=colrecv.at[stage, 1 - side],
            send_sem=col_send.at[stage, side],
            recv_sem=col_recv.at[stage, side],
            device_id=(sec, a, b - 1 if side == 0 else b + 1),
            device_id_type=MESH,
        )

    row_ok = (a > 0, a < n_gx - 1)
    col_ok = (b > 0, b < n_gy - 1)

    def send_rows(stage, buf):
        for side in range(2):

            @pl.when(row_ok[side])
            def _(side=side):
                row_copy(stage, buf, side).start()

    def send_cols(stage):
        for side in range(2):

            @pl.when(col_ok[side])
            def _(side=side):
                col_copy(stage, side).start()

    def wait_halo(stage, buf):
        for side in range(2):

            @pl.when(col_ok[side])
            def _(side=side):
                col_copy(stage, 1 - side).wait_recv()

        for side in range(2):

            @pl.when(row_ok[side])
            def _(side=side):
                row_copy(stage, buf, 1 - side).wait_recv()

    def wait_sent(stage, buf):
        for side in range(2):

            @pl.when(col_ok[side])
            def _(side=side):
                col_copy(stage, side).wait_send()

            @pl.when(row_ok[side])
            def _(side=side):
                row_copy(stage, buf, side).wait_send()

    lane = iota((levels, LANES), 1)

    def flat(buf, f):
        return [buf.at[f, i].reshape(levels * rows, LANES) for i in range(tiles)]

    flat_raw = [flat(raw, f) for f in range(3)]
    flat_out = [flat(out, f) for f in range(3)]

    def column(f, x):
        parts = [ref[pl.ds(x, levels, stride=rows), :] for ref in flat_raw[f]]
        return jnp.concatenate(parts, axis=1)

    def put(f, x, value):
        for i, ref in enumerate(flat_out[f]):
            ref[pl.ds(x, levels, stride=rows), :] = value[:, i * LANES : (i + 1) * LANES]

    def loaded(f):
        for i in range(tiles):
            load(f, i).wait()

    def pack(value, x, carry):
        low, high = carry
        low = jnp.where(lane == x, pltpu.roll(value[:, :LANES], x, 1), low)
        high = jnp.where(lane == x, pltpu.roll(value[:, width - LANES :], x + 1, 1), high)
        return low, high

    def along_y(value, stage, x):
        left = pltpu.roll(colrecv[stage, 0], lax.rem(LANES - x, LANES), 1)
        right = pltpu.roll(colrecv[stage, 1], LANES - 1 - x, 1)
        plus = pltpu.roll(value, width - 1, 1)
        minus = pltpu.roll(value, 1, 1)
        end = jnp.where(lane == LANES - 1, right, plus[:, width - LANES :])
        start = jnp.where(lane == 0, left, minus[:, :LANES])
        plus = jnp.concatenate([plus[:, : width - LANES], end], axis=1)
        minus = jnp.concatenate([start, minus[:, LANES:]], axis=1)
        return plus - minus

    m_high, m_low = split(vertical[0], 2)
    m_high, m_low = m_high.astype(F32), m_low.astype(F32)
    mixer = jnp.concatenate([m_high, m_high, m_low, m_low], axis=1).astype(BF16)

    def mix(right_side):
        high, low = split(right_side, 2)
        return right_side + dot(mixer, jnp.concatenate([high, low, high, low], axis=0))

    def pressure_row(stage, x, p, u_buf, v):
        divergence = (u_buf[x + 2] - u_buf[x]) + along_y(v, stage, x)
        return mix(p - speed[0, pl.ds(x, 1), :] * divergence)

    def sweep(row, after_edges, carry):
        carry = lax.fori_loop(0, 2, lambda i, c: row(i * (rows - 1), c), carry)
        after_edges()
        carry = lax.fori_loop(
            0, (rows - 2) // 2, lambda i, c: row(2 * i + 2, row(2 * i + 1, c)), carry
        )
        return carry

    blank = jnp.zeros((levels, LANES), F32)
    pair = (blank, blank)

    def start_cols(stage, carry):
        colsend[stage, 0] = carry[0]
        colsend[stage, 1] = carry[1]
        send_cols(stage)

    loaded(1)
    u0[1] = column(1, 0)
    u0[rows] = column(1, rows - 1)
    pl.semaphore_wait(barrier, 2 * n_gx - 1 + beside)
    send_rows(0, u0)
    loaded(2)
    start_cols(0, lax.fori_loop(0, rows, lambda x, c: pack(column(2, x), x, c), pair))
    loaded(0)

    def wide_row(value):
        return value[0, 0].reshape(1, pairs).astype(F32)

    diagonal = iota((pairs, pairs), 0) == iota((pairs, pairs), 1)

    def upright(row):
        return jnp.sum(jnp.where(diagonal, row, 0.0), axis=1, keepdims=True)

    slots = n_gx * out_blocks
    shift = out_blocks.bit_length() - 1

    def slot_key(index):
        within = block_key(index & (out_blocks - 1), rows, out_per_row)
        return ((index >> shift) * out_blocks + within).astype(F32)

    tile_col = tile_in[0, 0].astype(F32)
    target_row = wide_row(target_in)

    def y_copy(t):
        return pltpu.make_async_remote_copy(
            src_ref=ybuf.at[t],
            dst_ref=yrecv.at[a],
            send_sem=y_send.at[t],
            recv_sem=y_recv.at[a],
            device_id=(1, t, b),
            device_id_type=MESH,
        )

    def x_copy():
        return pltpu.make_async_remote_copy(
            src_ref=xbuf,
            dst_ref=xbuf,
            send_sem=x_send,
            recv_sem=x_recv,
            device_id=(0, a, b),
            device_id_type=MESH,
        )

    def t_copy(t):
        return pltpu.make_async_remote_copy(
            src_ref=trecv.at[a],
            dst_ref=trecv.at[a],
            send_sem=t_send.at[t],
            recv_sem=t_recv.at[a],
            device_id=(1, t, b),
            device_id_type=MESH,
        )

    def wide(j):
        return jnp.concatenate([wbuf[j], wbuf[j + 1]], axis=1)

    @pl.when(sec == 0)
    def _():
        drivers = [
            jnp.concatenate([raw[f, i, 0] for i in range(tiles)], axis=1) for f in range(3)
        ] + [temp[0]]
        heat = jnp.zeros((rows, width), F32)
        for f in range(coef.shape[0]):
            total = coef[f, 0] * drivers[0]
            for k in range(1, 4):
                total = total + coef[f, k] * drivers[k]
            heat = heat + gain[f] * jnp.tanh(total).astype(BF16).astype(F32)
        blocks = jnp.concatenate(
            [heat[:, i * in_width : (i + 1) * in_width] for i in range(in_per_row)], axis=0
        )
        source_col = upright(wide_row(source_in))
        key = block_key(iota((pairs, in_blocks), 1), rows, in_per_row).astype(F32)
        picking = (source_col == key).astype(F32).astype(BF16)
        high, low = [dot(picking, piece) for piece in split(blocks, 2)]
        sub = iota((8, out_width), 0)
        groups = []
        for g in range(pairs // 8):
            if g % (per_chunk // 8) == 0:
                load_weights(g * 8 // per_chunk).wait()
            part = slice(8 * g, 8 * g + 8)
            left = jnp.concatenate([high[part], low[part]], axis=0).astype(BF16)
            group = jnp.zeros((8, out_width), F32)
            for i in range(0, 8, 2):
                both = dot(left, wide(8 * g + i))
                both = both[:8] + both[8:]
                group = jnp.where(sub == i, both[:, :out_width], group)
                group = jnp.where(sub == i + 1, both[:, out_width:], group)
            groups.append(group)
        heated = jnp.concatenate(groups, axis=0)
        tile_row = jnp.sum(jnp.where(diagonal, tile_col, 0.0), axis=0, keepdims=True)
        slot_row = tile_row * out_blocks + target_row
        placing = (slot_key(iota((slots, pairs), 0)) == slot_row).astype(F32).astype(BF16)
        dense = sum(dot(placing, piece) for piece in split(heated, 3))
        ybuf[...] = dense.reshape(n_gx, out_blocks, out_width)
        for t in range(n_gx):
            y_copy(t).start()

    def fill(x, c):
        u0[x + 1] = column(1, x)
        return c

    lax.fori_loop(1, rows - 1, fill, 0)
    wait_halo(0, u0)

    def first_pressure(x, c):
        p = pressure_row(0, x, column(0, x), u0, column(2, x))
        p1[x + 1] = p
        return pack(p, x, c)

    start_cols(1, sweep(first_pressure, lambda: send_rows(1, p1), pair))
    wait_halo(1, p1)

    def free(x):
        return mask[0, pl.ds(x, 1), :].astype(F32)

    def first_velocity(x, c):
        w = free(x)
        u1[x + 1] = w * (u0[x + 1] - 0.5 * (p1[x + 2] - p1[x]))
        v = w * (column(2, x) - 0.5 * along_y(p1[x + 1], 1, x))
        v1[x] = v
        return pack(v, x, c)

    start_cols(2, sweep(first_velocity, lambda: send_rows(2, u1), pair))

    def as_blocks(value):
        return jnp.concatenate(
            [value[:, i * out_width : (i + 1) * out_width] for i in range(out_per_row)], axis=0
        )

    @pl.when(sec == 1)
    def _():
        heating = jnp.zeros((out_blocks, out_width), F32)
        for t in range(n_gx):
            pltpu.make_async_remote_copy(
                src_ref=ybuf.at[t],
                dst_ref=yrecv.at[t],
                send_sem=y_send.at[t],
                recv_sem=y_recv.at[t],
                device_id=(0, t, b),
                device_id_type=MESH,
            ).wait_recv()
            heating = heating + yrecv[t]
        ocean = as_blocks(temp[0]) + as_blocks(mask[0].astype(F32)) * heating
        trecv[a] = ocean.astype(BF16)
        for t in range(n_gx):

            @pl.when(t != a)
            def _():
                t_copy(t).start()

        surface[0] = jnp.concatenate(
            [ocean[i * rows : (i + 1) * rows] for i in range(out_per_row)], axis=1
        )

    wait_halo(2, u1)

    def second_pressure(x, c):
        p = pressure_row(2, x, p1[x + 1], u1, v1[x])
        p2[x + 1] = p
        put(0, x, p)
        return pack(p, x, c)

    start_cols(3, sweep(second_pressure, lambda: send_rows(3, p2), pair))

    def store(f, i):
        part = final.at[0, f, :, :, pl.ds(i * LANES, LANES)]
        return pltpu.make_async_copy(out.at[f, i], part, out_sem.at[f, i])

    def store_all(f):
        for i in range(tiles):
            store(f, i).start()

    store_all(0)

    @pl.when(sec == 1)
    def _():
        for i in range(CHUNKS):
            load_weights(i).wait()
        for t in range(n_gx):

            @pl.when(t != a)
            def _():
                pltpu.make_async_remote_copy(
                    src_ref=trecv.at[t],
                    dst_ref=trecv.at[t],
                    send_sem=t_send.at[t],
                    recv_sem=t_recv.at[t],
                    device_id=(1, t, b),
                    device_id_type=MESH,
                ).wait_recv()

        slot_col = tile_col * out_blocks + upright(target_row)
        picking = (slot_key(iota((pairs, slots), 1)) == slot_col).astype(F32).astype(BF16)
        returned = dot(picking, trecv[...].reshape(slots, out_width))
        key = block_key(iota((in_blocks, out_width), 0), rows, in_per_row)
        total = jnp.zeros((in_blocks, in_width), F32)
        for j in range(0, pairs, 2):
            left = jnp.concatenate(
                [
                    jnp.where(key == source_s[0, 0, i], returned[i : i + 1], 0.0)
                    for i in (j, j + 1)
                ],
                axis=1,
            ).astype(BF16)
            total = total + lax.dot_general(
                left, wide(j), (((1,), (1,)), ((), ())), preferred_element_type=F32
            )
        xbuf[...] = jnp.concatenate(
            [total[i * rows : (i + 1) * rows] for i in range(in_per_row)], axis=1
        )
        x_copy().start()

    wait_halo(3, p2)

    def second_velocity(x, c):
        w = free(x)
        put(1, x, w * (u1[x + 1] - 0.5 * (p2[x + 2] - p2[x])))
        put(2, x, w * (v1[x] - 0.5 * along_y(p2[x + 1], 3, x)))
        return c

    sweep(second_velocity, lambda: None, 0)
    store_all(1)
    store_all(2)

    for stage, buf in enumerate((u0, p1, u1, p2)):
        wait_sent(stage, buf)

    @pl.when(sec == 0)
    def _():
        for t in range(n_gx):
            y_copy(t).wait_send()
        x_copy().wait_recv()
        surface[0] = xbuf[...]

    @pl.when(sec == 1)
    def _():
        for t in range(n_gx):

            @pl.when(t != a)
            def _():
                t_copy(t).wait_send()

        x_copy().wait_send()

    for f in range(3):
        for i in range(tiles):
            store(f, i).wait()


def local(n_gx, n_gy, *args):
    state, speed, mask, vertical, temp, coef, gain, tile, source, target, weights = args
    _, fields, levels, rows, width = state.shape
    pairs, in_width, out_width = weights.shape[2:]
    out_blocks = rows * width // out_width
    vmem = pl.BlockSpec(memory_space=pltpu.VMEM)
    smem = pl.BlockSpec(memory_space=pltpu.SMEM)
    hbm = pl.BlockSpec(memory_space=pl.ANY)
    dma = pltpu.SemaphoreType.DMA
    tiled = pltpu.VMEM((fields, width // LANES, levels, rows, LANES), F32)
    tall = pltpu.VMEM((rows + 2, levels, width), F32)
    return pl.pallas_call(
        functools.partial(kernel, n_gx, n_gy),
        out_shape=(
            jax.ShapeDtypeStruct(state.shape, F32),
            jax.ShapeDtypeStruct(temp.shape, F32),
        ),
        in_specs=[hbm, vmem, vmem, vmem, vmem, smem, smem, vmem, vmem, vmem, smem, hbm],
        out_specs=(hbm, vmem),
        scratch_shapes=[
            tiled,
            tiled,
            pltpu.VMEM((pairs, in_width, out_width), BF16),
            tall,
            tall,
            tall,
            pltpu.VMEM((rows, levels, width), F32),
            tall,
            pltpu.VMEM((4, 2, levels, LANES), F32),
            pltpu.VMEM((4, 2, levels, LANES), F32),
            pltpu.VMEM((n_gx, out_blocks, out_width), F32),
            pltpu.VMEM((n_gx, out_blocks, out_width), F32),
            pltpu.VMEM((n_gx, out_blocks, out_width), BF16),
            pltpu.VMEM((rows, width), F32),
            dma((fields, width // LANES)),
            dma((CHUNKS,)),
            dma((4, 2)),
            dma((4, 2)),
            dma((4, 2)),
            dma((4, 2)),
            dma((n_gx,)),
            dma((n_gx,)),
            dma((n_gx,)),
            dma((n_gx,)),
            dma(()),
            dma(()),
            dma((fields, width // LANES)),
        ],
        compiler_params=pltpu.CompilerParams(
            collective_id=0, has_side_effects=True, vmem_limit_bytes=40 * 2**20
        ),
    )(state, speed, mask, vertical, temp, coef, gain, tile, source, target, source, weights)


def solution(mesh):
    return jax.shard_map(
        functools.partial(local, mesh.shape["gx"], mesh.shape["gy"]),
        mesh=mesh,
        in_specs=(
            P("sec", None, None, "gx", "gy"),
            P("sec", "gx", "gy"),
            P("sec", "gx", "gy"),
            P("sec", None, None),
            P("sec", "gx", "gy"),
            P(),
            P(),
            P("gx", "gy", None, None),
            P("gx", "gy", None),
            P("gx", "gy", None),
            P("gx", "gy", None, None, None),
        ),
        out_specs=(P("sec", None, None, "gx", "gy"), P("sec", "gx", "gy")),
        check_vma=False,
    )
```

```python
import functools

import jax
import jax.numpy as jnp
from jax import lax
from jax.experimental import pallas as pl
from jax.experimental.pallas import tpu as pltpu
from jax.sharding import PartitionSpec as P

MESH = pl.DeviceIdType.MESH
F32 = jnp.float32
BF16 = jnp.bfloat16
LANES = 128
CHUNKS = 8


def iota(shape, axis):
    return lax.broadcasted_iota(jnp.int32, shape, axis)


def split(value, parts):
    pieces = []
    for _ in range(parts):
        piece = value.astype(BF16)
        pieces.append(piece)
        value = value - piece.astype(F32)
    return pieces


def dot(a, b):
    return jnp.dot(a, b, preferred_element_type=F32)


def block_key(index, rows, per_row):
    return (index & (rows - 1)) * per_row + (index >> (rows.bit_length() - 1))


def kernel(
    n_gx,
    n_gy,
    state,
    speed_in,
    mask_in,
    vertical_in,
    temp_in,
    coef_in,
    gain_in,
    tile_hbm,
    source_hbm,
    target_hbm,
    weights,
    final,
    surface,
    speed,
    mask,
    vertical,
    temp,
    coef,
    gain,
    tile_in,
    source_in,
    target_in,
    raw,
    out,
    wbuf,
    u0,
    p1,
    u1,
    v1,
    p2,
    rowsend,
    rowrecv,
    colsend,
    colrecv,
    ybuf,
    yrecv,
    trecv,
    xbuf,
    sbuf,
    load_sem,
    small_sem,
    surface_sem,
    w_sem,
    row_send,
    row_recv,
    col_send,
    col_recv,
    y_send,
    y_recv,
    t_send,
    t_recv,
    x_send,
    x_recv,
    out_sem,
):
    sec = lax.axis_index("sec")
    a = lax.axis_index("gx")
    b = lax.axis_index("gy")
    levels, rows, width = state.shape[2:]
    tiles = width // LANES
    pairs, in_width, out_width = wbuf.shape
    in_per_row = width // in_width
    out_per_row = width // out_width
    in_blocks = rows * in_per_row
    out_blocks = rows * out_per_row
    per_chunk = pairs // CHUNKS

    def load(f, i):
        part = state.at[0, f, :, :, pl.ds(i * LANES, LANES)]
        return pltpu.make_async_copy(part, raw.at[f, i], load_sem.at[f, i])

    def load_weights(i):
        part = pl.ds(i * per_chunk, per_chunk)
        return pltpu.make_async_copy(weights.at[0, 0, part], wbuf.at[part], w_sem.at[i])

    small = [
        pltpu.make_async_copy(src, dst, small_sem.at[i])
        for i, (src, dst) in enumerate(
            (
                (speed_in, speed),
                (mask_in, mask),
                (vertical_in, vertical),
                (temp_in, temp),
                (coef_in, coef),
                (gain_in, gain),
                (tile_hbm, tile_in),
                (source_hbm, source_in),
                (target_hbm, target_in),
            )
        )
    ]
    for f in (1, 2):
        for i in range(tiles):
            load(f, i).start()
    for copy in small:
        copy.start()
    for i in range(tiles):
        load(0, i).start()
    for i in range(CHUNKS):
        load_weights(i).start()

    barrier = pltpu.get_barrier_semaphore()
    for s in range(2):
        for t in range(n_gx):

            @pl.when(jnp.logical_or(s != sec, t != a))
            def _():
                pl.semaphore_signal(barrier, inc=1, device_id=(s, t, b), device_id_type=MESH)

    @pl.when(b > 0)
    def _():
        pl.semaphore_signal(barrier, inc=1, device_id=(sec, a, b - 1), device_id_type=MESH)

    @pl.when(b < n_gy - 1)
    def _():
        pl.semaphore_signal(barrier, inc=1, device_id=(sec, a, b + 1), device_id_type=MESH)

    beside = (b > 0).astype(jnp.int32) + (b < n_gy - 1).astype(jnp.int32)

    @pl.when(a == 0)
    def _():
        for buf in (u0, p1, u1, p2):
            buf[0] = jnp.zeros((levels, width), F32)

    @pl.when(a == n_gx - 1)
    def _():
        for buf in (u0, p1, u1, p2):
            buf[rows + 1] = jnp.zeros((levels, width), F32)

    @pl.when(b == 0)
    def _():
        for stage in range(4):
            colrecv[stage, 0] = jnp.zeros((levels, LANES), F32)

    @pl.when(b == n_gy - 1)
    def _():
        for stage in range(4):
            colrecv[stage, 1] = jnp.zeros((levels, LANES), F32)

    def row_copy(stage, side):
        return pltpu.make_async_remote_copy(
            src_ref=rowsend.at[stage, side],
            dst_ref=rowrecv.at[stage, 1 - side],
            send_sem=row_send.at[stage, side],
            recv_sem=row_recv.at[stage, side],
            device_id=(sec, a - 1 if side == 0 else a + 1, b),
            device_id_type=MESH,
        )

    def col_copy(stage, side):
        return pltpu.make_async_remote_copy(
            src_ref=colsend.at[stage, side],
            dst_ref=colrecv.at[stage, 1 - side],
            send_sem=col_send.at[stage, side],
            recv_sem=col_recv.at[stage, side],
            device_id=(sec, a, b - 1 if side == 0 else b + 1),
            device_id_type=MESH,
        )

    row_ok = (a > 0, a < n_gx - 1)
    col_ok = (b > 0, b < n_gy - 1)

    def send_rows(stage, buf):
        for side in range(2):

            @pl.when(row_ok[side])
            def _(side=side):
                rowsend[stage, side] = buf[rows if side else 1].astype(BF16)
                row_copy(stage, side).start()

    def send_cols(stage):
        for side in range(2):

            @pl.when(col_ok[side])
            def _(side=side):
                col_copy(stage, side).start()

    def wait_halo(stage, buf):
        for side in range(2):

            @pl.when(col_ok[side])
            def _(side=side):
                col_copy(stage, 1 - side).wait_recv()

        for side in range(2):

            @pl.when(row_ok[side])
            def _(side=side):
                row_copy(stage, 1 - side).wait_recv()
                buf[rows + 1 if side else 0] = rowrecv[stage, side].astype(F32)

    def wait_sent(stage):
        for side in range(2):

            @pl.when(col_ok[side])
            def _(side=side):
                col_copy(stage, side).wait_send()

            @pl.when(row_ok[side])
            def _(side=side):
                row_copy(stage, side).wait_send()

    lane = iota((levels, LANES), 1)

    def flat(buf, f):
        return [buf.at[f, i].reshape(levels * rows, LANES) for i in range(tiles)]

    flat_raw = [flat(raw, f) for f in range(3)]
    flat_out = [flat(out, f) for f in range(3)]

    def column(f, x):
        parts = [ref[pl.ds(x, levels, stride=rows), :] for ref in flat_raw[f]]
        return jnp.concatenate(parts, axis=1)

    def put(f, x, value):
        for i, ref in enumerate(flat_out[f]):
            ref[pl.ds(x, levels, stride=rows), :] = value[:, i * LANES : (i + 1) * LANES]

    def loaded(f):
        for i in range(tiles):
            load(f, i).wait()

    def pack(value, x, carry):
        low, high = carry
        low = jnp.where(lane == x, pltpu.roll(value[:, :LANES], x, 1), low)
        high = jnp.where(lane == x, pltpu.roll(value[:, width - LANES :], x + 1, 1), high)
        return low, high

    def along_y(value, stage, x):
        left = pltpu.roll(colrecv[stage, 0], lax.rem(LANES - x, LANES), 1)
        right = pltpu.roll(colrecv[stage, 1], LANES - 1 - x, 1)
        plus = pltpu.roll(value, width - 1, 1)
        minus = pltpu.roll(value, 1, 1)
        end = jnp.where(lane == LANES - 1, right, plus[:, width - LANES :])
        start = jnp.where(lane == 0, left, minus[:, :LANES])
        plus = jnp.concatenate([plus[:, : width - LANES], end], axis=1)
        minus = jnp.concatenate([start, minus[:, LANES:]], axis=1)
        return plus - minus

    def mix(right_side):
        high, low = split(right_side, 2)
        return right_side + dot(mixer, jnp.concatenate([high, low, high, low], axis=0))

    def pressure_row(stage, x, p, u_buf, v):
        divergence = (u_buf[x + 2] - u_buf[x]) + along_y(v, stage, x)
        return mix(p - speed[0, pl.ds(x, 1), :] * divergence)

    def sweep(row, after_edges, carry):
        carry = lax.fori_loop(0, 2, lambda i, c: row(i * (rows - 1), c), carry)
        after_edges()
        inner = rows - 2
        step = next(k for k in (7, 6, 5, 4, 3, 2, 1) if inner % k == 0)

        def several(i, c):
            for k in range(step):
                c = row(i * step + 1 + k, c)
            return c

        return lax.fori_loop(0, inner // step, several, carry)

    blank = jnp.zeros((levels, LANES), F32)
    pair = (blank, blank)

    def start_cols(stage, carry):
        colsend[stage, 0] = carry[0]
        colsend[stage, 1] = carry[1]
        send_cols(stage)

    loaded(1)
    u0[1] = column(1, 0)
    u0[rows] = column(1, rows - 1)
    pl.semaphore_wait(barrier, 2 * n_gx - 1 + beside)
    send_rows(0, u0)
    loaded(2)
    start_cols(0, lax.fori_loop(0, rows, lambda x, c: pack(column(2, x), x, c), pair))
    for copy in small:
        copy.wait()
    m_high, m_low = split(vertical[0], 2)
    m_high, m_low = m_high.astype(F32), m_low.astype(F32)
    mixer = jnp.concatenate([m_high, m_high, m_low, m_low], axis=1).astype(BF16)
    loaded(0)

    def wide_row(value):
        return value[0, 0].reshape(1, pairs).astype(F32)

    diagonal = iota((pairs, pairs), 0) == iota((pairs, pairs), 1)

    def upright(row):
        return jnp.sum(jnp.where(diagonal, row, 0.0), axis=1, keepdims=True)

    slots = n_gx * out_blocks
    shift = out_blocks.bit_length() - 1

    def slot_key(index):
        within = block_key(index & (out_blocks - 1), rows, out_per_row)
        return ((index >> shift) * out_blocks + within).astype(F32)

    slot_row = wide_row(tile_in) * out_blocks + wide_row(target_in)

    def y_copy(t):
        return pltpu.make_async_remote_copy(
            src_ref=ybuf.at[t],
            dst_ref=yrecv.at[a],
            send_sem=y_send.at[t],
            recv_sem=y_recv.at[a],
            device_id=(1, t, b),
            device_id_type=MESH,
        )

    def x_copy():
        return pltpu.make_async_remote_copy(
            src_ref=xbuf,
            dst_ref=xbuf,
            send_sem=x_send,
            recv_sem=x_recv,
            device_id=(0, a, b),
            device_id_type=MESH,
        )

    def t_copy(t):
        return pltpu.make_async_remote_copy(
            src_ref=trecv.at[a],
            dst_ref=trecv.at[a],
            send_sem=t_send.at[t],
            recv_sem=t_recv.at[a],
            device_id=(1, t, b),
            device_id_type=MESH,
        )

    def wide(j):
        return jnp.concatenate([wbuf[j], wbuf[j + 1]], axis=1)

    @pl.when(sec == 0)
    def _():
        drivers = [
            jnp.concatenate([raw[f, i, 0] for i in range(tiles)], axis=1) for f in range(3)
        ] + [temp[0]]
        heat = jnp.zeros((rows, width), F32)
        factors, gains = coef[...], gain[...]
        for f in range(factors.shape[1]):
            total = factors[0:1, f : f + 1] * drivers[0]
            for k in range(1, 4):
                total = total + factors[k : k + 1, f : f + 1] * drivers[k]
            heat = heat + gains[:, f : f + 1] * jnp.tanh(total).astype(BF16).astype(F32)
        blocks = jnp.concatenate(
            [heat[:, i * in_width : (i + 1) * in_width] for i in range(in_per_row)], axis=0
        )
        source_col = upright(wide_row(source_in))
        key = block_key(iota((pairs, in_blocks), 1), rows, in_per_row).astype(F32)
        picking = (source_col == key).astype(F32).astype(BF16)
        high, low = [dot(picking, piece) for piece in split(blocks, 2)]
        sub = iota((8, out_width), 0)
        groups = []
        for g in range(pairs // 8):
            if g % (per_chunk // 8) == 0:
                load_weights(g * 8 // per_chunk).wait()
            part = slice(8 * g, 8 * g + 8)
            left = jnp.concatenate([high[part], low[part]], axis=0).astype(BF16)
            group = jnp.zeros((8, out_width), F32)
            for i in range(0, 8, 2):
                both = dot(left, wide(8 * g + i))
                both = both[:8] + both[8:]
                group = jnp.where(sub == i, both[:, :out_width], group)
                group = jnp.where(sub == i + 1, both[:, out_width:], group)
            groups.append(group)
        heated = jnp.concatenate(groups, axis=0)
        placing = (slot_key(iota((slots, pairs), 0)) == slot_row).astype(F32).astype(BF16)
        dense = sum(dot(placing, piece) for piece in split(heated, 3))
        ybuf[...] = dense.astype(BF16).reshape(n_gx, out_blocks, out_width)
        for t in range(n_gx):
            y_copy(t).start()

    def fill(x, c):
        u0[x + 1] = column(1, x)
        return c

    lax.fori_loop(1, rows - 1, fill, 0)
    wait_halo(0, u0)

    def first_pressure(x, c):
        p = pressure_row(0, x, column(0, x), u0, column(2, x))
        p1[x + 1] = p
        return pack(p, x, c)

    start_cols(1, sweep(first_pressure, lambda: send_rows(1, p1), pair))
    wait_halo(1, p1)

    def free(x):
        return mask[0, pl.ds(x, 1), :].astype(F32)

    def first_velocity(x, c):
        w = free(x)
        u1[x + 1] = w * (u0[x + 1] - 0.5 * (p1[x + 2] - p1[x]))
        v = w * (column(2, x) - 0.5 * along_y(p1[x + 1], 1, x))
        v1[x] = v
        return pack(v, x, c)

    start_cols(2, sweep(first_velocity, lambda: send_rows(2, u1), pair))

    def as_blocks(value):
        return jnp.concatenate(
            [value[:, i * out_width : (i + 1) * out_width] for i in range(out_per_row)], axis=0
        )

    @pl.when(sec == 1)
    def _():
        heating = jnp.zeros((out_blocks, out_width), F32)
        for t in range(n_gx):
            pltpu.make_async_remote_copy(
                src_ref=ybuf.at[t],
                dst_ref=yrecv.at[t],
                send_sem=y_send.at[t],
                recv_sem=y_recv.at[t],
                device_id=(0, t, b),
                device_id_type=MESH,
            ).wait_recv()
            heating = heating + yrecv[t].astype(F32)
        ocean = as_blocks(temp[0]) + as_blocks(mask[0].astype(F32)) * heating
        trecv[a] = ocean.astype(BF16)
        for t in range(n_gx):

            @pl.when(t != a)
            def _():
                t_copy(t).start()

        sbuf[...] = jnp.concatenate(
            [ocean[i * rows : (i + 1) * rows] for i in range(out_per_row)], axis=1
        )

    wait_halo(2, u1)

    def second_pressure(x, c):
        p = pressure_row(2, x, p1[x + 1], u1, v1[x])
        p2[x + 1] = p
        put(0, x, p)
        return pack(p, x, c)

    start_cols(3, sweep(second_pressure, lambda: send_rows(3, p2), pair))

    def store(f, i):
        part = final.at[0, f, :, :, pl.ds(i * LANES, LANES)]
        return pltpu.make_async_copy(out.at[f, i], part, out_sem.at[f, i])

    def store_all(f):
        for i in range(tiles):
            store(f, i).start()

    store_all(0)

    @pl.when(sec == 1)
    def _():
        for i in range(CHUNKS):
            load_weights(i).wait()
        for t in range(n_gx):

            @pl.when(t != a)
            def _():
                pltpu.make_async_remote_copy(
                    src_ref=trecv.at[t],
                    dst_ref=trecv.at[t],
                    send_sem=t_send.at[t],
                    recv_sem=t_recv.at[t],
                    device_id=(1, t, b),
                    device_id_type=MESH,
                ).wait_recv()

        slot_col = upright(slot_row)
        picking = (slot_key(iota((pairs, slots), 1)) == slot_col).astype(F32).astype(BF16)
        returned = dot(picking, trecv[...].reshape(slots, out_width))
        key = block_key(iota((in_blocks, pairs), 0), rows, in_per_row).astype(F32)
        owner = (key == wide_row(source_in)).astype(F32)
        total = jnp.zeros((in_blocks, in_width), F32)
        for j in range(0, pairs, 2):
            left = jnp.concatenate(
                [
                    owner[:, i : i + 1] * returned[i : i + 1]
                    for i in (j, j + 1)
                ],
                axis=1,
            ).astype(BF16)
            total = total + lax.dot_general(
                left, wide(j), (((1,), (1,)), ((), ())), preferred_element_type=F32
            )
        xbuf[...] = jnp.concatenate(
            [total[i * rows : (i + 1) * rows] for i in range(in_per_row)], axis=1
        )
        x_copy().start()

    wait_halo(3, p2)

    def second_velocity(x, c):
        w = free(x)
        put(1, x, w * (u1[x + 1] - 0.5 * (p2[x + 2] - p2[x])))
        put(2, x, w * (v1[x] - 0.5 * along_y(p2[x + 1], 3, x)))
        return c

    sweep(second_velocity, lambda: None, 0)
    store_all(1)
    store_all(2)

    for stage in range(4):
        wait_sent(stage)

    @pl.when(sec == 0)
    def _():
        for t in range(n_gx):
            y_copy(t).wait_send()
        x_copy().wait_recv()
        sbuf[...] = xbuf[...]

    @pl.when(sec == 1)
    def _():
        for t in range(n_gx):

            @pl.when(t != a)
            def _():
                t_copy(t).wait_send()

        x_copy().wait_send()

    surface_copy = pltpu.make_async_copy(sbuf, surface.at[0], surface_sem)
    surface_copy.start()
    for f in range(3):
        for i in range(tiles):
            store(f, i).wait()
    surface_copy.wait()


def local(n_gx, n_gy, *args):
    state, speed, mask, vertical, temp, coef, gain, tile, source, target, weights = args
    coef = coef.T
    gain = gain.reshape(1, -1)
    tile = tile.reshape(source.shape)
    _, fields, levels, rows, width = state.shape
    pairs, in_width, out_width = weights.shape[2:]
    out_blocks = rows * width // out_width
    hbm = pl.BlockSpec(memory_space=pltpu.HBM)
    free = pl.BlockSpec(memory_space=pl.ANY)
    dma = pltpu.SemaphoreType.DMA
    tiled = pltpu.VMEM((fields, width // LANES, levels, rows, LANES), F32)
    tall = pltpu.VMEM((rows + 2, levels, width), F32)
    return pl.pallas_call(
        functools.partial(kernel, n_gx, n_gy),
        out_shape=(
            jax.ShapeDtypeStruct(state.shape, F32),
            jax.ShapeDtypeStruct(temp.shape, F32),
        ),
        in_specs=[hbm] * 11,
        out_specs=(free, free),
        scratch_shapes=[
            pltpu.VMEM(speed.shape, F32),
            pltpu.VMEM(mask.shape, jnp.int32),
            pltpu.VMEM(vertical.shape, F32),
            pltpu.VMEM(temp.shape, F32),
            pltpu.VMEM(coef.shape, F32),
            pltpu.VMEM(gain.shape, F32),
            pltpu.VMEM(tile.shape, jnp.int32),
            pltpu.VMEM(source.shape, jnp.int32),
            pltpu.VMEM(target.shape, jnp.int32),
            tiled,
            tiled,
            pltpu.VMEM((pairs, in_width, out_width), BF16),
            tall,
            tall,
            tall,
            pltpu.VMEM((rows, levels, width), F32),
            tall,
            pltpu.VMEM((4, 2, levels, width), BF16),
            pltpu.VMEM((4, 2, levels, width), BF16),
            pltpu.VMEM((4, 2, levels, LANES), F32),
            pltpu.VMEM((4, 2, levels, LANES), F32),
            pltpu.VMEM((n_gx, out_blocks, out_width), BF16),
            pltpu.VMEM((n_gx, out_blocks, out_width), BF16),
            pltpu.VMEM((n_gx, out_blocks, out_width), BF16),
            pltpu.VMEM((rows, width), F32),
            pltpu.VMEM((rows, width), F32),
            dma((fields, width // LANES)),
            dma((9,)),
            dma(()),
            dma((CHUNKS,)),
            dma((4, 2)),
            dma((4, 2)),
            dma((4, 2)),
            dma((4, 2)),
            dma((n_gx,)),
            dma((n_gx,)),
            dma((n_gx,)),
            dma((n_gx,)),
            dma(()),
            dma(()),
            dma((fields, width // LANES)),
        ],
        compiler_params=pltpu.CompilerParams(
            collective_id=0, has_side_effects=True, vmem_limit_bytes=62 * 2**20
        ),
    )(state, speed, mask, vertical, temp, coef, gain, tile, source, target, weights)


def solution(mesh):
    return jax.shard_map(
        functools.partial(local, mesh.shape["gx"], mesh.shape["gy"]),
        mesh=mesh,
        in_specs=(
            P("sec", None, None, "gx", "gy"),
            P("sec", "gx", "gy"),
            P("sec", "gx", "gy"),
            P("sec", None, None),
            P("sec", "gx", "gy"),
            P(),
            P(),
            P("gx", "gy", None, None),
            P("gx", "gy", None),
            P("gx", "gy", None),
            P("gx", "gy", None, None, None),
        ),
        out_specs=(P("sec", None, None, "gx", "gy"), P("sec", "gx", "gy")),
        check_vma=False,
    )
```

```python
import functools

import jax
import jax.numpy as jnp
from jax import lax
from jax.experimental import pallas as pl
from jax.experimental.pallas import tpu as pltpu
from jax.sharding import PartitionSpec as P

MESH = pl.DeviceIdType.MESH
F32 = jnp.float32
BF16 = jnp.bfloat16
LANES = 128
CHUNKS = 8
STAGES = 4
MARGIN = 4
P_FIELD, U_FIELD, V_FIELD = 0, 1, 2
SPEED, MASK, P_COLS, V_COLS, U_COLS, U_BEFORE, U_AFTER = range(7)


def iota(shape, axis):
    return lax.broadcasted_iota(jnp.int32, shape, axis)


def split(value, parts):
    pieces = []
    for _ in range(parts):
        piece = value.astype(BF16)
        pieces.append(piece)
        value = value - piece.astype(F32)
    return pieces


def dot(a, b):
    return jnp.dot(a, b, preferred_element_type=F32)


def block_key(index, rows, per_row):
    return (index & (rows - 1)) * per_row + (index >> (rows.bit_length() - 1))


def kernel(
    n_gx,
    n_gy,
    state,
    speed_in,
    mask_in,
    vertical_in,
    temp_in,
    coef_in,
    gain_in,
    tile_hbm,
    source_hbm,
    target_hbm,
    weights,
    p2_out,
    u1_out,
    v1_out,
    surface,
    speed,
    mask,
    vertical,
    temp,
    coef,
    gain,
    tile_in,
    source_in,
    target_in,
    raw,
    wbuf,
    u0,
    p1,
    u1,
    v1,
    p2,
    p_ext,
    v_ext,
    c_wide,
    w_wide,
    rowsend,
    rowrecv,
    colsend,
    u_recv,
    v_recv,
    p_recv,
    speed_recv,
    mask_recv,
    ybuf,
    yrecv,
    trecv,
    xbuf,
    sbuf,
    load_sem,
    small_sem,
    surface_sem,
    w_sem,
    row_send,
    row_recv,
    col_send,
    col_recv,
    y_send,
    y_recv,
    t_send,
    t_recv,
    x_send,
    x_recv,
    out_sem,
):
    sec = lax.axis_index("sec")
    a = lax.axis_index("gx")
    b = lax.axis_index("gy")
    levels, rows, width = state.shape[2:]
    tiles = width // LANES
    pairs, in_width, out_width = wbuf.shape
    in_per_row = width // in_width
    out_per_row = width // out_width
    in_blocks = rows * in_per_row
    out_blocks = rows * out_per_row
    per_chunk = pairs // CHUNKS

    def load(f, i):
        part = state.at[0, f, :, :, pl.ds(i * LANES, LANES)]
        return pltpu.make_async_copy(part, raw.at[f, i], load_sem.at[f, i])

    def load_weights(i):
        part = pl.ds(i * per_chunk, per_chunk)
        return pltpu.make_async_copy(weights.at[0, 0, part], wbuf.at[part], w_sem.at[i])

    small = [
        pltpu.make_async_copy(src, dst, small_sem.at[i])
        for i, (src, dst) in enumerate(
            (
                (speed_in, speed),
                (mask_in, mask),
                (vertical_in, vertical),
                (temp_in, temp),
                (coef_in, coef),
                (gain_in, gain),
                (tile_hbm, tile_in),
                (source_hbm, source_in),
                (target_hbm, target_in),
            )
        )
    ]
    for f in (1, 2):
        for i in range(tiles):
            load(f, i).start()
    for copy in small:
        copy.start()
    for i in range(tiles):
        load(0, i).start()
    for i in range(CHUNKS):
        load_weights(i).start()

    barrier = pltpu.get_barrier_semaphore()
    for s in range(2):
        for t in range(n_gx):

            @pl.when(jnp.logical_or(s != sec, t != a))
            def _():
                pl.semaphore_signal(barrier, inc=1, device_id=(s, t, b), device_id_type=MESH)

    row_ok = (a > 0, a < n_gx - 1)
    col_ok = (b > 0, b < n_gy - 1)
    both_ok = [[jnp.logical_and(r, c) for c in col_ok] for r in row_ok]

    for side in range(2):
        for dx in (-1, 0, 1):
            near = col_ok[side] if dx == 0 else both_ok[(dx + 1) // 2][side]

            @pl.when(near)
            def _(side=side, dx=dx):
                pl.semaphore_signal(
                    barrier,
                    inc=1,
                    device_id=(sec, a + dx, b + 2 * side - 1),
                    device_id_type=MESH,
                )

    beside = (b > 0).astype(jnp.int32) + (b < n_gy - 1).astype(jnp.int32)
    beside = beside * (1 + (a > 0).astype(jnp.int32) + (a < n_gx - 1).astype(jnp.int32))

    for side in range(2):

        @pl.when(jnp.logical_not(row_ok[side]))
        def _(side=side):
            for buf in (u0, p1, u1, p2):
                buf[side * (rows + 1)] = jnp.zeros(buf.shape[1:], F32)
            for other in range(2):
                u_recv[2 * side, other] = jnp.zeros((levels, LANES), F32)

        @pl.when(jnp.logical_not(col_ok[side]))
        def _(side=side):
            for dx in range(3):
                u_recv[dx, side] = jnp.zeros((levels, LANES), F32)
            v_recv[side] = jnp.zeros((levels, LANES), F32)
            p_recv[side] = jnp.zeros((levels, LANES), F32)
            speed_recv[side] = jnp.zeros((rows, LANES), F32)
            mask_recv[side] = jnp.zeros((rows, LANES), jnp.int32)

    def row_copy(stage, side):
        src, dst = rowsend.at[stage, side], rowrecv.at[stage, 1 - side]
        if stage == 0:
            src, dst = src.at[:, pl.ds(0, width)], dst.at[:, pl.ds(0, width)]
        return pltpu.make_async_remote_copy(
            src_ref=src,
            dst_ref=dst,
            send_sem=row_send.at[stage, side],
            recv_sem=row_recv.at[stage, side],
            device_id=(sec, a - 1 if side == 0 else a + 1, b),
            device_id_type=MESH,
        )

    def col_copy(kind, side):
        edge = pl.ds(0 if side == 0 else width - LANES, LANES)
        other = 1 - side
        src, dst = {
            SPEED: (speed.at[0, :, edge], speed_recv.at[other]),
            MASK: (mask.at[0, :, edge], mask_recv.at[other]),
            P_COLS: (colsend.at[P_FIELD, side], p_recv.at[other]),
            V_COLS: (colsend.at[V_FIELD, side], v_recv.at[other]),
            U_COLS: (colsend.at[U_FIELD, side], u_recv.at[1, other]),
            U_BEFORE: (colsend.at[U_FIELD, side], u_recv.at[2, other]),
            U_AFTER: (colsend.at[U_FIELD, side], u_recv.at[0, other]),
        }[kind]
        to = {U_BEFORE: a - 1, U_AFTER: a + 1}.get(kind, a)
        return pltpu.make_async_remote_copy(
            src_ref=src,
            dst_ref=dst,
            send_sem=col_send.at[kind, side],
            recv_sem=col_recv.at[kind, side],
            device_id=(sec, to, b - 1 if side == 0 else b + 1),
            device_id_type=MESH,
        )

    def col_sends(kind, side):
        return {U_BEFORE: both_ok[0], U_AFTER: both_ok[1]}.get(kind, col_ok)[side]

    def col_comes(kind, side):
        return {U_BEFORE: both_ok[1], U_AFTER: both_ok[0]}.get(kind, col_ok)[side]

    def send_rows(stage, buf):
        span = width if stage == 0 else width + LANES
        for side in range(2):

            @pl.when(row_ok[side])
            def _(side=side):
                edge = buf[rows if side else 1]
                rowsend[stage, side, :, :span] = edge[:, :span].astype(BF16)
                row_copy(stage, side).start()

    def send_cols(*kinds):
        for kind in kinds:
            for side in range(2):

                @pl.when(col_sends(kind, side))
                def _(side=side, kind=kind):
                    col_copy(kind, side).start()

    def wait_cols():
        for kind in range(7):
            for side in range(2):

                @pl.when(col_comes(kind, side))
                def _(side=side, kind=kind):
                    col_copy(kind, 1 - side).wait_recv()

    def wait_rows(stage, buf):
        for side in range(2):

            @pl.when(row_ok[side])
            def _(side=side):
                row_copy(stage, 1 - side).wait_recv()
                at = rows + 1 if side else 0
                if stage == 0:
                    buf[at, :, :width] = rowrecv[stage, side, :, :width].astype(F32)
                    near = u_recv.at[2 * side]
                    buf[at, :, width:] = margin(near, 0 if side else rows - 1)
                else:
                    buf[at] = rowrecv[stage, side].astype(F32)

    def wait_sent():
        for side in range(2):
            for kind in range(7):

                @pl.when(col_sends(kind, side))
                def _(side=side, kind=kind):
                    col_copy(kind, side).wait_send()

            for stage in range(STAGES):

                @pl.when(row_ok[side])
                def _(side=side, stage=stage):
                    row_copy(stage, side).wait_send()

    lane = iota((levels, LANES), 1)

    def flat(buf, f):
        return [buf.at[f, i].reshape(levels * rows, LANES) for i in range(tiles)]

    flat_raw = [flat(raw, f) for f in range(3)]

    def column(f, x):
        parts = [ref[pl.ds(x, levels, stride=rows), :] for ref in flat_raw[f]]
        return jnp.concatenate(parts, axis=1)

    def edges(f, x):
        return [flat_raw[f][i][pl.ds(x, levels, stride=rows), :] for i in (0, tiles - 1)]

    def loaded(f):
        for i in range(tiles):
            load(f, i).wait()

    mine = lane // MARGIN

    def pack(f, x, carry):
        low, high = carry
        first, last = edges(f, x)
        low = jnp.where(mine == x, pltpu.roll(first, MARGIN * x, 1), low)
        high = jnp.where(mine == x, pltpu.roll(last, MARGIN * x + MARGIN, 1), high)
        return low, high

    def pack_all(f):
        blank = jnp.zeros((levels, LANES), F32)

        def several(i, carry):
            for k in range(4):
                carry = pack(f, 4 * i + k, carry)
            return carry

        low, high = lax.fori_loop(0, rows // 4, several, (blank, blank))
        colsend[f, 0] = low
        colsend[f, 1] = high

    def margin(ref, x):
        before = pltpu.roll(ref[0], LANES - MARGIN - MARGIN * x, 1)
        after = pltpu.roll(ref[1], lax.rem(LANES - MARGIN * x, LANES), 1)
        rest = jnp.where(lane >= LANES - MARGIN, before, 0.0)
        return jnp.where(lane < MARGIN, after, rest)

    def along_y(value):
        return pltpu.roll(value, value.shape[1] - 1, 1) - pltpu.roll(value, 1, 1)

    def mix(right_side):
        high, low = split(right_side, 2)
        return right_side + dot(mixer, jnp.concatenate([high, low, high, low], axis=0))

    def pressure_row(x, p, u_buf, v):
        divergence = (u_buf[x + 2] - u_buf[x]) + along_y(v)
        return mix(p - c_wide[pl.ds(x, 1), :] * divergence)

    def sweep(row, after_edges):
        def edge(i, c):
            row(i * (rows - 1))
            return c

        lax.fori_loop(0, 2, edge, 0)
        after_edges()
        inner = rows - 2
        step = next(k for k in (7, 6, 5, 4, 3, 2, 1) if inner % k == 0)

        def several(i, c):
            for k in range(step):
                row(i * step + 1 + k)
            return c

        lax.fori_loop(0, inner // step, several, 0)

    loaded(U_FIELD)
    u0[1, :, :width] = column(U_FIELD, 0)
    u0[rows, :, :width] = column(U_FIELD, rows - 1)
    pl.semaphore_wait(barrier, 2 * n_gx - 1 + beside)
    send_rows(0, u0)
    pack_all(U_FIELD)
    send_cols(U_COLS, U_BEFORE, U_AFTER)
    loaded(V_FIELD)
    pack_all(V_FIELD)
    send_cols(V_COLS)
    for copy in small:
        copy.wait()
    send_cols(SPEED, MASK)
    loaded(P_FIELD)
    pack_all(P_FIELD)
    send_cols(P_COLS)
    m_high, m_low = split(vertical[0], 2)
    m_high, m_low = m_high.astype(F32), m_low.astype(F32)
    mixer = jnp.concatenate([m_high, m_high, m_low, m_low], axis=1).astype(BF16)

    def wide_row(value):
        return value[0, 0].reshape(1, pairs).astype(F32)

    diagonal = iota((pairs, pairs), 0) == iota((pairs, pairs), 1)

    def upright(row):
        return jnp.sum(jnp.where(diagonal, row, 0.0), axis=1, keepdims=True)

    slots = n_gx * out_blocks
    shift = out_blocks.bit_length() - 1

    def slot_key(index):
        within = block_key(index & (out_blocks - 1), rows, out_per_row)
        return ((index >> shift) * out_blocks + within).astype(F32)

    slot_row = wide_row(tile_in) * out_blocks + wide_row(target_in)

    def y_copy(t):
        return pltpu.make_async_remote_copy(
            src_ref=ybuf.at[t],
            dst_ref=yrecv.at[a],
            send_sem=y_send.at[t],
            recv_sem=y_recv.at[a],
            device_id=(1, t, b),
            device_id_type=MESH,
        )

    def x_copy():
        return pltpu.make_async_remote_copy(
            src_ref=xbuf,
            dst_ref=xbuf,
            send_sem=x_send,
            recv_sem=x_recv,
            device_id=(0, a, b),
            device_id_type=MESH,
        )

    def t_copy(t):
        return pltpu.make_async_remote_copy(
            src_ref=trecv.at[a],
            dst_ref=trecv.at[a],
            send_sem=t_send.at[t],
            recv_sem=t_recv.at[a],
            device_id=(1, t, b),
            device_id_type=MESH,
        )

    def wide(j):
        return jnp.concatenate([wbuf[j], wbuf[j + 1]], axis=1)

    @pl.when(sec == 0)
    def _():
        drivers = [
            jnp.concatenate([raw[f, i, 0] for i in range(tiles)], axis=1) for f in range(3)
        ] + [temp[0]]
        heat = jnp.zeros((rows, width), F32)
        factors, gains = coef[...], gain[...]
        for f in range(factors.shape[1]):
            total = factors[0:1, f : f + 1] * drivers[0]
            for k in range(1, 4):
                total = total + factors[k : k + 1, f : f + 1] * drivers[k]
            heat = heat + gains[:, f : f + 1] * jnp.tanh(total).astype(BF16).astype(F32)
        blocks = jnp.concatenate(
            [heat[:, i * in_width : (i + 1) * in_width] for i in range(in_per_row)], axis=0
        )
        source_col = upright(wide_row(source_in))
        key = block_key(iota((pairs, in_blocks), 1), rows, in_per_row).astype(F32)
        picking = (source_col == key).astype(F32).astype(BF16)
        high, low = [dot(picking, piece) for piece in split(blocks, 2)]
        sub = iota((8, out_width), 0)
        groups = []
        for g in range(pairs // 8):
            if g % (per_chunk // 8) == 0:
                load_weights(g * 8 // per_chunk).wait()
            part = slice(8 * g, 8 * g + 8)
            left = jnp.concatenate([high[part], low[part]], axis=0).astype(BF16)
            group = jnp.zeros((8, out_width), F32)
            for i in range(0, 8, 2):
                both = dot(left, wide(8 * g + i))
                both = both[:8] + both[8:]
                group = jnp.where(sub == i, both[:, :out_width], group)
                group = jnp.where(sub == i + 1, both[:, out_width:], group)
            groups.append(group)
        heated = jnp.concatenate(groups, axis=0)
        placing = (slot_key(iota((slots, pairs), 0)) == slot_row).astype(F32).astype(BF16)
        dense = sum(dot(placing, piece) for piece in split(heated, 3))
        ybuf[...] = dense.astype(BF16).reshape(n_gx, out_blocks, out_width)
        for t in range(n_gx):
            y_copy(t).start()

    def fill(x, c):
        u0[x + 1, :, :width] = column(U_FIELD, x)
        return c

    lax.fori_loop(1, rows - 1, fill, 0)
    wait_cols()

    def fill_margins(x, c):
        u0[x + 1, :, width:] = margin(u_recv.at[1], x)
        v_ext[x] = margin(v_recv, x)
        p_ext[x] = margin(p_recv, x)
        return c

    lax.fori_loop(0, rows, fill_margins, 0)
    across = iota((rows, LANES), 1)

    def around(pair):
        rest = jnp.where(across >= LANES - MARGIN, pair[0], 0.0)
        return jnp.where(across < MARGIN, pair[1], rest)

    c_wide[:, :width] = speed[0]
    c_wide[:, width:] = around(speed_recv[...])
    w_wide[:, :width] = mask[0].astype(F32)
    w_wide[:, width:] = around(mask_recv[...].astype(F32))
    wait_rows(0, u0)

    def wide_column(f, ext, x):
        return jnp.concatenate([column(f, x), ext[x]], axis=1)

    def first_pressure(x):
        p = wide_column(P_FIELD, p_ext, x)
        p1[x + 1] = pressure_row(x, p, u0, wide_column(V_FIELD, v_ext, x))

    sweep(first_pressure, lambda: send_rows(1, p1))
    wait_rows(1, p1)

    def first_velocity(x):
        w = w_wide[pl.ds(x, 1), :]
        u1[x + 1] = w * (u0[x + 1] - 0.5 * (p1[x + 2] - p1[x]))
        v1[x] = w * (wide_column(V_FIELD, v_ext, x) - 0.5 * along_y(p1[x + 1]))

    sweep(first_velocity, lambda: send_rows(2, u1))

    near = pl.ds(0, width)
    inner = pl.ds(1, rows)
    stores = [
        pltpu.make_async_copy(u1.at[inner, :, near], u1_out, out_sem.at[0]),
        pltpu.make_async_copy(v1.at[:, :, near], v1_out, out_sem.at[1]),
        pltpu.make_async_copy(p2.at[inner], p2_out.at[inner], out_sem.at[2]),
        pltpu.make_async_copy(p2.at[0], p2_out.at[0], out_sem.at[3]),
        pltpu.make_async_copy(p2.at[rows + 1], p2_out.at[rows + 1], out_sem.at[4]),
    ]
    stores[0].start()
    stores[1].start()

    def as_blocks(value):
        return jnp.concatenate(
            [value[:, i * out_width : (i + 1) * out_width] for i in range(out_per_row)], axis=0
        )

    @pl.when(sec == 1)
    def _():
        heating = jnp.zeros((out_blocks, out_width), F32)
        for t in range(n_gx):
            pltpu.make_async_remote_copy(
                src_ref=ybuf.at[t],
                dst_ref=yrecv.at[t],
                send_sem=y_send.at[t],
                recv_sem=y_recv.at[t],
                device_id=(0, t, b),
                device_id_type=MESH,
            ).wait_recv()
            heating = heating + yrecv[t].astype(F32)
        ocean = as_blocks(temp[0]) + as_blocks(mask[0].astype(F32)) * heating
        trecv[a] = ocean.astype(BF16)
        for t in range(n_gx):

            @pl.when(t != a)
            def _():
                t_copy(t).start()

        sbuf[...] = jnp.concatenate(
            [ocean[i * rows : (i + 1) * rows] for i in range(out_per_row)], axis=1
        )

    wait_rows(2, u1)

    def second_pressure(x):
        p2[x + 1] = pressure_row(x, p1[x + 1], u1, v1[x])

    sweep(second_pressure, lambda: send_rows(3, p2))
    stores[2].start()

    @pl.when(sec == 1)
    def _():
        for i in range(CHUNKS):
            load_weights(i).wait()
        for t in range(n_gx):

            @pl.when(t != a)
            def _():
                pltpu.make_async_remote_copy(
                    src_ref=trecv.at[t],
                    dst_ref=trecv.at[t],
                    send_sem=t_send.at[t],
                    recv_sem=t_recv.at[t],
                    device_id=(1, t, b),
                    device_id_type=MESH,
                ).wait_recv()

        slot_col = upright(slot_row)
        picking = (slot_key(iota((pairs, slots), 1)) == slot_col).astype(F32).astype(BF16)
        returned = dot(picking, trecv[...].reshape(slots, out_width))
        key = block_key(iota((in_blocks, pairs), 0), rows, in_per_row).astype(F32)
        owner = (key == wide_row(source_in)).astype(F32)
        total = jnp.zeros((in_blocks, in_width), F32)
        for j in range(0, pairs, 2):
            left = jnp.concatenate(
                [
                    owner[:, i : i + 1] * returned[i : i + 1]
                    for i in (j, j + 1)
                ],
                axis=1,
            ).astype(BF16)
            total = total + lax.dot_general(
                left, wide(j), (((1,), (1,)), ((), ())), preferred_element_type=F32
            )
        xbuf[...] = jnp.concatenate(
            [total[i * rows : (i + 1) * rows] for i in range(in_per_row)], axis=1
        )
        x_copy().start()

    wait_rows(3, p2)
    stores[3].start()
    stores[4].start()
    wait_sent()

    @pl.when(sec == 0)
    def _():
        for t in range(n_gx):
            y_copy(t).wait_send()
        x_copy().wait_recv()
        sbuf[...] = xbuf[...]

    @pl.when(sec == 1)
    def _():
        for t in range(n_gx):

            @pl.when(t != a)
            def _():
                t_copy(t).wait_send()

        x_copy().wait_send()

    surface_copy = pltpu.make_async_copy(sbuf, surface.at[0], surface_sem)
    surface_copy.start()
    for copy in stores:
        copy.wait()
    surface_copy.wait()


def last_kernel(
    p_in,
    u_in,
    v_in,
    mask_in,
    surface_in,
    final,
    surface,
    p,
    u,
    v,
    mask,
    out,
    sem,
    out_sem,
    small_sem,
):
    rows, levels, width = u_in.shape
    tiles = width // LANES
    parts = rows // 4
    half = 8

    mask_copy = pltpu.make_async_copy(mask_in, mask, small_sem.at[0])
    surface_copy = pltpu.make_async_copy(surface_in, surface, small_sem.at[1])
    mask_copy.start()
    loads = []
    for k in range(parts):
        first = 0 if k == 0 else 4 * k + 2
        p_rows = pl.ds(first, 4 * k + 6 - first)
        part = pl.ds(4 * k, 4)
        loads.append(
            [
                pltpu.make_async_copy(src, dst, sem.at[k, i])
                for i, (src, dst) in enumerate(
                    (
                        (p_in.at[p_rows], p.at[p_rows]),
                        (u_in.at[part], u.at[part]),
                        (v_in.at[part], v.at[part]),
                    )
                )
            ]
        )
        for copy in loads[-1]:
            copy.start()
    surface_copy.start()
    mask_copy.wait()

    def store(h, f, i):
        part = final.at[0, f, :, pl.ds(h * half, half), pl.ds(i * LANES, LANES)]
        return pltpu.make_async_copy(out.at[h, f, i], part, out_sem.at[h, f, i])

    stores = [store(h, f, i) for h in range(rows // half) for f in range(3) for i in range(tiles)]
    for k in range(parts):
        for copy in loads[k]:
            copy.wait()
        for x in range(4 * k, 4 * k + 4):
            h = x // half
            w = mask[0, x : x + 1, :].astype(F32)
            here = p[x + 1]
            span = here.shape[1]
            plus = pltpu.roll(here, span - 1, 1)[:, :width]
            minus = pltpu.roll(here, 1, 1)[:, :width]
            gradient = p[x + 2, :, :width] - p[x, :, :width]
            values = (
                here[:, :width],
                w * (u[x] - 0.5 * gradient),
                w * (v[x] - 0.5 * (plus - minus)),
            )
            for f, value in enumerate(values):
                for i in range(tiles):
                    flat = out.at[h, f, i].reshape(levels * half, LANES)
                    at = pl.ds(x % half, levels, stride=half)
                    flat[at, :] = value[:, i * LANES : (i + 1) * LANES]
        if (4 * k + 4) % half == 0:
            per_half = 3 * tiles
            h = (4 * k + 4) // half - 1
            for copy in stores[h * per_half : (h + 1) * per_half]:
                copy.start()
    for copy in stores:
        copy.wait()
    surface_copy.wait()


def local(n_gx, n_gy, *args):
    state, speed, mask, vertical, temp, coef, gain, tile, source, target, weights = args
    coef = coef.T
    gain = gain.reshape(1, -1)
    tile = tile.reshape(source.shape)
    _, fields, levels, rows, width = state.shape
    pairs, in_width, out_width = weights.shape[2:]
    out_blocks = rows * width // out_width
    hbm = pl.BlockSpec(memory_space=pltpu.HBM)
    free = pl.BlockSpec(memory_space=pl.ANY)
    dma = pltpu.SemaphoreType.DMA
    tiled = pltpu.VMEM((fields, width // LANES, levels, rows, LANES), F32)
    span = width + LANES
    tall = pltpu.VMEM((rows + 2, levels, span), F32)
    ext = pltpu.VMEM((rows, levels, LANES), F32)
    params = dict(has_side_effects=True, vmem_limit_bytes=62 * 2**20)
    p2, u1, v1, surface = pl.pallas_call(
        functools.partial(kernel, n_gx, n_gy),
        out_shape=(
            jax.ShapeDtypeStruct((rows + 2, levels, span), F32),
            jax.ShapeDtypeStruct((rows, levels, width), F32),
            jax.ShapeDtypeStruct((rows, levels, width), F32),
            jax.ShapeDtypeStruct(temp.shape, F32),
        ),
        in_specs=[hbm] * 11,
        out_specs=(free,) * 4,
        scratch_shapes=[
            pltpu.VMEM(speed.shape, F32),
            pltpu.VMEM(mask.shape, jnp.int32),
            pltpu.VMEM(vertical.shape, F32),
            pltpu.VMEM(temp.shape, F32),
            pltpu.VMEM(coef.shape, F32),
            pltpu.VMEM(gain.shape, F32),
            pltpu.VMEM(tile.shape, jnp.int32),
            pltpu.VMEM(source.shape, jnp.int32),
            pltpu.VMEM(target.shape, jnp.int32),
            tiled,
            pltpu.VMEM((pairs, in_width, out_width), BF16),
            tall,
            tall,
            tall,
            pltpu.VMEM((rows, levels, span), F32),
            tall,
            ext,
            ext,
            pltpu.VMEM((rows, span), F32),
            pltpu.VMEM((rows, span), F32),
            pltpu.VMEM((STAGES, 2, levels, span), BF16),
            pltpu.VMEM((STAGES, 2, levels, span), BF16),
            pltpu.VMEM((fields, 2, levels, LANES), F32),
            pltpu.VMEM((3, 2, levels, LANES), F32),
            pltpu.VMEM((2, levels, LANES), F32),
            pltpu.VMEM((2, levels, LANES), F32),
            pltpu.VMEM((2, rows, LANES), F32),
            pltpu.VMEM((2, rows, LANES), jnp.int32),
            pltpu.VMEM((n_gx, out_blocks, out_width), BF16),
            pltpu.VMEM((n_gx, out_blocks, out_width), BF16),
            pltpu.VMEM((n_gx, out_blocks, out_width), BF16),
            pltpu.VMEM((rows, width), F32),
            pltpu.VMEM((rows, width), F32),
            dma((fields, width // LANES)),
            dma((9,)),
            dma(()),
            dma((CHUNKS,)),
            dma((STAGES, 2)),
            dma((STAGES, 2)),
            dma((7, 2)),
            dma((7, 2)),
            dma((n_gx,)),
            dma((n_gx,)),
            dma((n_gx,)),
            dma((n_gx,)),
            dma(()),
            dma(()),
            dma((5,)),
        ],
        compiler_params=pltpu.CompilerParams(collective_id=0, **params),
    )(state, speed, mask, vertical, temp, coef, gain, tile, source, target, weights)
    return pl.pallas_call(
        last_kernel,
        out_shape=(
            jax.ShapeDtypeStruct(state.shape, F32),
            jax.ShapeDtypeStruct(temp.shape, F32),
        ),
        in_specs=[hbm] * 5,
        out_specs=(free, free),
        scratch_shapes=[
            tall,
            pltpu.VMEM((rows, levels, width), F32),
            pltpu.VMEM((rows, levels, width), F32),
            pltpu.VMEM(mask.shape, jnp.int32),
            pltpu.VMEM((rows // 8, fields, width // LANES, levels, 8, LANES), F32),
            dma((rows // 4, 3)),
            dma((rows // 8, fields, width // LANES)),
            dma((2,)),
        ],
        compiler_params=pltpu.CompilerParams(**params),
    )(p2, u1, v1, mask, surface)


def solution(mesh):
    return jax.shard_map(
        functools.partial(local, mesh.shape["gx"], mesh.shape["gy"]),
        mesh=mesh,
        in_specs=(
            P("sec", None, None, "gx", "gy"),
            P("sec", "gx", "gy"),
            P("sec", "gx", "gy"),
            P("sec", None, None),
            P("sec", "gx", "gy"),
            P(),
            P(),
            P("gx", "gy", None, None),
            P("gx", "gy", None),
            P("gx", "gy", None),
            P("gx", "gy", None, None, None),
        ),
        out_specs=(P("sec", None, None, "gx", "gy"), P("sec", "gx", "gy")),
        check_vma=False,
    )
```

```python
import functools

import jax
import jax.numpy as jnp
from jax import lax
from jax.experimental import pallas as pl
from jax.experimental.pallas import tpu as pltpu
from jax.sharding import PartitionSpec as P

MESH = pl.DeviceIdType.MESH
F32 = jnp.float32
BF16 = jnp.bfloat16
LANES = 128
CHUNKS = 8
STAGES = 4
MARGIN = 4
P_FIELD, U_FIELD, V_FIELD = 0, 1, 2
SPEED, MASK, P_COLS, V_COLS, U_COLS, U_BEFORE, U_AFTER = range(7)


def iota(shape, axis):
    return lax.broadcasted_iota(jnp.int32, shape, axis)


def split(value, parts):
    pieces = []
    for _ in range(parts):
        piece = value.astype(BF16)
        pieces.append(piece)
        value = value - piece.astype(F32)
    return pieces


def dot(a, b):
    return jnp.dot(a, b, preferred_element_type=F32)


def block_key(index, rows, per_row):
    return (index & (rows - 1)) * per_row + (index >> (rows.bit_length() - 1))


def wide_row(ref):
    return ref[0, 0].reshape(1, ref.shape[-1]).astype(F32)


def upright(row):
    size = row.shape[1]
    diagonal = iota((size, size), 0) == iota((size, size), 1)
    return jnp.sum(jnp.where(diagonal, row, 0.0), axis=1, keepdims=True)


def slot_key(index, blocks, rows, per_row):
    within = block_key(index & (blocks - 1), rows, per_row)
    return ((index >> (blocks.bit_length() - 1)) * blocks + within).astype(F32)


def wide(weights, j):
    return jnp.concatenate([weights[j], weights[j + 1]], axis=1)


def kernel(
    n_gx,
    n_gy,
    state,
    speed_in,
    mask_in,
    vertical_in,
    temp_in,
    coef_in,
    gain_in,
    tile_hbm,
    source_hbm,
    target_hbm,
    weights,
    p2_out,
    u1_out,
    v1_out,
    surface,
    returned,
    speed,
    mask,
    vertical,
    temp,
    coef,
    gain,
    tile_in,
    source_in,
    target_in,
    raw,
    wbuf,
    u0,
    p1,
    u1,
    v1,
    p2,
    p_ext,
    v_ext,
    c_wide,
    w_wide,
    rowsend,
    rowrecv,
    colsend,
    u_recv,
    v_recv,
    p_recv,
    speed_recv,
    mask_recv,
    ybuf,
    yrecv,
    tsend,
    trecv,
    sbuf,
    load_sem,
    small_sem,
    surface_sem,
    w_sem,
    row_send,
    row_recv,
    col_send,
    col_recv,
    y_send,
    y_recv,
    t_send,
    t_recv,
    out_sem,
):
    sec = lax.axis_index("sec")
    a = lax.axis_index("gx")
    b = lax.axis_index("gy")
    levels, rows, width = state.shape[2:]
    tiles = width // LANES
    pairs, in_width, out_width = wbuf.shape
    in_per_row = width // in_width
    out_per_row = width // out_width
    in_blocks = rows * in_per_row
    out_blocks = rows * out_per_row
    per_chunk = pairs // CHUNKS

    def load(f, i):
        part = state.at[0, f, :, :, pl.ds(i * LANES, LANES)]
        return pltpu.make_async_copy(part, raw.at[f, i], load_sem.at[f, i])

    def load_weights(i):
        part = pl.ds(i * per_chunk, per_chunk)
        return pltpu.make_async_copy(weights.at[0, 0, part], wbuf.at[part], w_sem.at[i])

    small = [
        pltpu.make_async_copy(src, dst, small_sem.at[i])
        for i, (src, dst) in enumerate(
            (
                (speed_in, speed),
                (mask_in, mask),
                (vertical_in, vertical),
                (temp_in, temp),
                (coef_in, coef),
                (gain_in, gain),
                (tile_hbm, tile_in),
                (source_hbm, source_in),
                (target_hbm, target_in),
            )
        )
    ]
    for f in (1, 2):
        for i in range(tiles):
            load(f, i).start()
    for copy in small:
        copy.start()
    for i in range(tiles):
        load(0, i).start()

    @pl.when(sec == 0)
    def _():
        for i in range(CHUNKS):
            load_weights(i).start()

    barrier = pltpu.get_barrier_semaphore()
    for s in range(2):
        for t in range(n_gx):

            @pl.when(jnp.logical_or(s != sec, t != a))
            def _():
                pl.semaphore_signal(barrier, inc=1, device_id=(s, t, b), device_id_type=MESH)

    row_ok = (a > 0, a < n_gx - 1)
    col_ok = (b > 0, b < n_gy - 1)
    both_ok = [[jnp.logical_and(r, c) for c in col_ok] for r in row_ok]

    for side in range(2):
        for dx in (-1, 0, 1):
            near = col_ok[side] if dx == 0 else both_ok[(dx + 1) // 2][side]

            @pl.when(near)
            def _(side=side, dx=dx):
                pl.semaphore_signal(
                    barrier,
                    inc=1,
                    device_id=(sec, a + dx, b + 2 * side - 1),
                    device_id_type=MESH,
                )

    beside = (b > 0).astype(jnp.int32) + (b < n_gy - 1).astype(jnp.int32)
    beside = beside * (1 + (a > 0).astype(jnp.int32) + (a < n_gx - 1).astype(jnp.int32))

    for side in range(2):

        @pl.when(jnp.logical_not(row_ok[side]))
        def _(side=side):
            for buf in (u0, p1, u1, p2):
                buf[side * (rows + 1)] = jnp.zeros(buf.shape[1:], F32)
            for other in range(2):
                u_recv[2 * side, other] = jnp.zeros((levels, LANES), F32)

        @pl.when(jnp.logical_not(col_ok[side]))
        def _(side=side):
            for dx in range(3):
                u_recv[dx, side] = jnp.zeros((levels, LANES), F32)
            v_recv[side] = jnp.zeros((levels, LANES), F32)
            p_recv[side] = jnp.zeros((levels, LANES), F32)
            speed_recv[side] = jnp.zeros((rows, LANES), F32)
            mask_recv[side] = jnp.zeros((rows, LANES), jnp.int32)

    def row_copy(stage, side):
        src, dst = rowsend.at[stage, side], rowrecv.at[stage, 1 - side]
        if stage == 0:
            src, dst = src.at[:, pl.ds(0, width)], dst.at[:, pl.ds(0, width)]
        return pltpu.make_async_remote_copy(
            src_ref=src,
            dst_ref=dst,
            send_sem=row_send.at[stage, side],
            recv_sem=row_recv.at[stage, side],
            device_id=(sec, a - 1 if side == 0 else a + 1, b),
            device_id_type=MESH,
        )

    def col_copy(kind, side):
        edge = pl.ds(0 if side == 0 else width - LANES, LANES)
        other = 1 - side
        src, dst = {
            SPEED: (speed.at[0, :, edge], speed_recv.at[other]),
            MASK: (mask.at[0, :, edge], mask_recv.at[other]),
            P_COLS: (colsend.at[P_FIELD, side], p_recv.at[other]),
            V_COLS: (colsend.at[V_FIELD, side], v_recv.at[other]),
            U_COLS: (colsend.at[U_FIELD, side], u_recv.at[1, other]),
            U_BEFORE: (colsend.at[U_FIELD, side], u_recv.at[2, other]),
            U_AFTER: (colsend.at[U_FIELD, side], u_recv.at[0, other]),
        }[kind]
        to = {U_BEFORE: a - 1, U_AFTER: a + 1}.get(kind, a)
        return pltpu.make_async_remote_copy(
            src_ref=src,
            dst_ref=dst,
            send_sem=col_send.at[kind, side],
            recv_sem=col_recv.at[kind, side],
            device_id=(sec, to, b - 1 if side == 0 else b + 1),
            device_id_type=MESH,
        )

    def col_sends(kind, side):
        return {U_BEFORE: both_ok[0], U_AFTER: both_ok[1]}.get(kind, col_ok)[side]

    def col_comes(kind, side):
        return {U_BEFORE: both_ok[1], U_AFTER: both_ok[0]}.get(kind, col_ok)[side]

    def send_rows(stage, buf):
        span = width if stage == 0 else width + LANES
        for side in range(2):

            @pl.when(row_ok[side])
            def _(side=side):
                edge = buf[rows if side else 1]
                rowsend[stage, side, :, :span] = edge[:, :span].astype(BF16)
                row_copy(stage, side).start()

    def send_cols(*kinds):
        for kind in kinds:
            for side in range(2):

                @pl.when(col_sends(kind, side))
                def _(side=side, kind=kind):
                    col_copy(kind, side).start()

    def wait_cols():
        for kind in range(7):
            for side in range(2):

                @pl.when(col_comes(kind, side))
                def _(side=side, kind=kind):
                    col_copy(kind, 1 - side).wait_recv()

    def wait_rows(stage, buf):
        for side in range(2):

            @pl.when(row_ok[side])
            def _(side=side):
                row_copy(stage, 1 - side).wait_recv()
                at = rows + 1 if side else 0
                if stage == 0:
                    buf[at, :, :width] = rowrecv[stage, side, :, :width].astype(F32)
                    near = u_recv.at[2 * side]
                    buf[at, :, width:] = margin(near, 0 if side else rows - 1)
                else:
                    buf[at] = rowrecv[stage, side].astype(F32)

    def wait_sent():
        for side in range(2):
            for kind in range(7):

                @pl.when(col_sends(kind, side))
                def _(side=side, kind=kind):
                    col_copy(kind, side).wait_send()

            for stage in range(STAGES):

                @pl.when(row_ok[side])
                def _(side=side, stage=stage):
                    row_copy(stage, side).wait_send()

    lane = iota((levels, LANES), 1)

    def flat(buf, f):
        return [buf.at[f, i].reshape(levels * rows, LANES) for i in range(tiles)]

    flat_raw = [flat(raw, f) for f in range(3)]

    def column(f, x):
        parts = [ref[pl.ds(x, levels, stride=rows), :] for ref in flat_raw[f]]
        return jnp.concatenate(parts, axis=1)

    def edges(f, x):
        return [flat_raw[f][i][pl.ds(x, levels, stride=rows), :] for i in (0, tiles - 1)]

    def loaded(f):
        for i in range(tiles):
            load(f, i).wait()

    mine = lane // MARGIN

    def pack(f, x, carry):
        low, high = carry
        first, last = edges(f, x)
        low = jnp.where(mine == x, pltpu.roll(first, MARGIN * x, 1), low)
        high = jnp.where(mine == x, pltpu.roll(last, MARGIN * x + MARGIN, 1), high)
        return low, high

    def pack_all(f):
        blank = jnp.zeros((levels, LANES), F32)

        def several(i, carry):
            for k in range(4):
                carry = pack(f, 4 * i + k, carry)
            return carry

        low, high = lax.fori_loop(0, rows // 4, several, (blank, blank))
        colsend[f, 0] = low
        colsend[f, 1] = high

    def margin(ref, x):
        before = pltpu.roll(ref[0], LANES - MARGIN - MARGIN * x, 1)
        after = pltpu.roll(ref[1], lax.rem(LANES - MARGIN * x, LANES), 1)
        rest = jnp.where(lane >= LANES - MARGIN, before, 0.0)
        return jnp.where(lane < MARGIN, after, rest)

    def along_y(value):
        return pltpu.roll(value, value.shape[1] - 1, 1) - pltpu.roll(value, 1, 1)

    def mix(right_side):
        high, low = split(right_side, 2)
        return right_side + dot(mixer, jnp.concatenate([high, low, high, low], axis=0))

    def pressure_row(x, p, u_buf, v):
        divergence = (u_buf[x + 2] - u_buf[x]) + along_y(v)
        return mix(p - c_wide[pl.ds(x, 1), :] * divergence)

    def sweep(row, after_edges):
        def edge(i, c):
            row(i * (rows - 1))
            return c

        lax.fori_loop(0, 2, edge, 0)
        after_edges()
        inner = rows - 2
        step = next(k for k in (7, 6, 5, 4, 3, 2, 1) if inner % k == 0)

        def several(i, c):
            for k in range(step):
                row(i * step + 1 + k)
            return c

        lax.fori_loop(0, inner // step, several, 0)

    loaded(U_FIELD)
    u0[1, :, :width] = column(U_FIELD, 0)
    u0[rows, :, :width] = column(U_FIELD, rows - 1)
    pl.semaphore_wait(barrier, 2 * n_gx - 1 + beside)
    send_rows(0, u0)
    pack_all(U_FIELD)
    send_cols(U_COLS, U_BEFORE, U_AFTER)
    loaded(V_FIELD)
    pack_all(V_FIELD)
    send_cols(V_COLS)
    for copy in small:
        copy.wait()
    send_cols(SPEED, MASK)
    loaded(P_FIELD)
    pack_all(P_FIELD)
    send_cols(P_COLS)
    m_high, m_low = split(vertical[0], 2)
    m_high, m_low = m_high.astype(F32), m_low.astype(F32)
    mixer = jnp.concatenate([m_high, m_high, m_low, m_low], axis=1).astype(BF16)

    slots = n_gx * out_blocks
    slot_row = wide_row(tile_in) * out_blocks + wide_row(target_in)

    def y_copy(t):
        return pltpu.make_async_remote_copy(
            src_ref=ybuf.at[t],
            dst_ref=yrecv.at[a],
            send_sem=y_send.at[t],
            recv_sem=y_recv.at[a],
            device_id=(1, t, b),
            device_id_type=MESH,
        )

    def t_copy(t):
        return pltpu.make_async_remote_copy(
            src_ref=tsend,
            dst_ref=trecv.at[a],
            send_sem=t_send.at[t],
            recv_sem=t_recv.at[a],
            device_id=(0, t, b),
            device_id_type=MESH,
        )

    @pl.when(sec == 0)
    def _():
        drivers = [
            jnp.concatenate([raw[f, i, 0] for i in range(tiles)], axis=1) for f in range(3)
        ] + [temp[0]]
        heat = jnp.zeros((rows, width), F32)
        factors, gains = coef[...], gain[...]
        for f in range(factors.shape[1]):
            total = factors[0:1, f : f + 1] * drivers[0]
            for k in range(1, 4):
                total = total + factors[k : k + 1, f : f + 1] * drivers[k]
            heat = heat + gains[:, f : f + 1] * jnp.tanh(total).astype(BF16).astype(F32)
        blocks = jnp.concatenate(
            [heat[:, i * in_width : (i + 1) * in_width] for i in range(in_per_row)], axis=0
        )
        source_col = upright(wide_row(source_in))
        key = block_key(iota((pairs, in_blocks), 1), rows, in_per_row).astype(F32)
        picking = (source_col == key).astype(F32).astype(BF16)
        high, low = [dot(picking, piece) for piece in split(blocks, 2)]
        sub = iota((8, out_width), 0)
        groups = []
        for g in range(pairs // 8):
            if g % (per_chunk // 8) == 0:
                load_weights(g * 8 // per_chunk).wait()
            part = slice(8 * g, 8 * g + 8)
            left = jnp.concatenate([high[part], low[part]], axis=0).astype(BF16)
            group = jnp.zeros((8, out_width), F32)
            for i in range(0, 8, 2):
                both = dot(left, wide(wbuf, 8 * g + i))
                both = both[:8] + both[8:]
                group = jnp.where(sub == i, both[:, :out_width], group)
                group = jnp.where(sub == i + 1, both[:, out_width:], group)
            groups.append(group)
        heated = jnp.concatenate(groups, axis=0)
        placing = (slot_key(iota((slots, pairs), 0), out_blocks, rows, out_per_row) == slot_row).astype(F32).astype(BF16)
        dense = sum(dot(placing, piece) for piece in split(heated, 3))
        ybuf[...] = dense.astype(BF16).reshape(n_gx, out_blocks, out_width)
        for t in range(n_gx):
            y_copy(t).start()

    def fill(x, c):
        u0[x + 1, :, :width] = column(U_FIELD, x)
        return c

    lax.fori_loop(1, rows - 1, fill, 0)
    wait_cols()

    def fill_margins(x, c):
        u0[x + 1, :, width:] = margin(u_recv.at[1], x)
        v_ext[x] = margin(v_recv, x)
        p_ext[x] = margin(p_recv, x)
        return c

    lax.fori_loop(0, rows, fill_margins, 0)
    across = iota((rows, LANES), 1)

    def around(pair):
        rest = jnp.where(across >= LANES - MARGIN, pair[0], 0.0)
        return jnp.where(across < MARGIN, pair[1], rest)

    c_wide[:, :width] = speed[0]
    c_wide[:, width:] = around(speed_recv[...])
    w_wide[:, :width] = mask[0].astype(F32)
    w_wide[:, width:] = around(mask_recv[...].astype(F32))
    wait_rows(0, u0)

    def wide_column(f, ext, x):
        return jnp.concatenate([column(f, x), ext[x]], axis=1)

    def first_pressure(x):
        p = wide_column(P_FIELD, p_ext, x)
        p1[x + 1] = pressure_row(x, p, u0, wide_column(V_FIELD, v_ext, x))

    sweep(first_pressure, lambda: send_rows(1, p1))
    wait_rows(1, p1)

    def first_velocity(x):
        w = w_wide[pl.ds(x, 1), :]
        u1[x + 1] = w * (u0[x + 1] - 0.5 * (p1[x + 2] - p1[x]))
        v1[x] = w * (wide_column(V_FIELD, v_ext, x) - 0.5 * along_y(p1[x + 1]))

    sweep(first_velocity, lambda: send_rows(2, u1))

    near = pl.ds(0, width)
    inner = pl.ds(1, rows)
    stores = [
        pltpu.make_async_copy(u1.at[inner, :, near], u1_out, out_sem.at[0]),
        pltpu.make_async_copy(v1.at[:, :, near], v1_out, out_sem.at[1]),
        pltpu.make_async_copy(p2.at[inner], p2_out.at[inner], out_sem.at[2]),
        pltpu.make_async_copy(p2.at[0], p2_out.at[0], out_sem.at[3]),
        pltpu.make_async_copy(p2.at[rows + 1], p2_out.at[rows + 1], out_sem.at[4]),
    ]
    stores[0].start()
    stores[1].start()

    def as_blocks(value):
        return jnp.concatenate(
            [value[:, i * out_width : (i + 1) * out_width] for i in range(out_per_row)], axis=0
        )

    @pl.when(sec == 1)
    def _():
        heating = jnp.zeros((out_blocks, out_width), F32)
        for t in range(n_gx):
            pltpu.make_async_remote_copy(
                src_ref=ybuf.at[t],
                dst_ref=yrecv.at[t],
                send_sem=y_send.at[t],
                recv_sem=y_recv.at[t],
                device_id=(0, t, b),
                device_id_type=MESH,
            ).wait_recv()
            heating = heating + yrecv[t].astype(F32)
        ocean = as_blocks(temp[0]) + as_blocks(mask[0].astype(F32)) * heating
        tsend[...] = ocean.astype(BF16)
        for t in range(n_gx):
            t_copy(t).start()

        sbuf[...] = jnp.concatenate(
            [ocean[i * rows : (i + 1) * rows] for i in range(out_per_row)], axis=1
        )

    wait_rows(2, u1)

    def second_pressure(x):
        p2[x + 1] = pressure_row(x, p1[x + 1], u1, v1[x])

    sweep(second_pressure, lambda: send_rows(3, p2))
    stores[2].start()

    wait_rows(3, p2)
    stores[3].start()
    stores[4].start()
    wait_sent()

    @pl.when(sec == 0)
    def _():
        for t in range(n_gx):
            y_copy(t).wait_send()
        for t in range(n_gx):
            pltpu.make_async_remote_copy(
                src_ref=tsend,
                dst_ref=trecv.at[t],
                send_sem=t_send.at[t],
                recv_sem=t_recv.at[t],
                device_id=(1, t, b),
                device_id_type=MESH,
            ).wait_recv()
        returned_copy = pltpu.make_async_copy(trecv, returned, surface_sem)
        returned_copy.start()
        returned_copy.wait()

    @pl.when(sec == 1)
    def _():
        surface_copy = pltpu.make_async_copy(sbuf, surface.at[0], surface_sem)
        surface_copy.start()
        for t in range(n_gx):
            t_copy(t).wait_send()
        surface_copy.wait()

    for copy in stores:
        copy.wait()


def last_kernel(
    p_in,
    u_in,
    v_in,
    mask_in,
    surface_in,
    returned_in,
    tile_hbm,
    source_hbm,
    target_hbm,
    weights,
    final,
    surface,
    p,
    u,
    v,
    mask,
    returned,
    tile_in,
    source_in,
    target_in,
    wbuf,
    sbuf,
    out,
    sem,
    out_sem,
    small_sem,
    w_sem,
):
    sec = lax.axis_index("sec")
    rows, levels, width = u_in.shape
    tiles = width // LANES
    parts = rows // 4
    half = 8

    mask_copy = pltpu.make_async_copy(mask_in, mask, small_sem.at[0])
    mask_copy.start()
    loads = []
    for k in range(parts):
        first = 0 if k == 0 else 4 * k + 2
        p_rows = pl.ds(first, 4 * k + 6 - first)
        part = pl.ds(4 * k, 4)
        loads.append(
            [
                pltpu.make_async_copy(src, dst, sem.at[k, i])
                for i, (src, dst) in enumerate(
                    (
                        (p_in.at[p_rows], p.at[p_rows]),
                        (u_in.at[part], u.at[part]),
                        (v_in.at[part], v.at[part]),
                    )
                )
            ]
        )
        for copy in loads[-1]:
            copy.start()
    small = [
        pltpu.make_async_copy(src, dst, small_sem.at[2 + i])
        for i, (src, dst) in enumerate(
            (
                (returned_in, returned),
                (tile_hbm, tile_in),
                (source_hbm, source_in),
                (target_hbm, target_in),
            )
        )
    ]
    pairs, in_width, out_width = wbuf.shape
    per_chunk = pairs // CHUNKS

    def load_weights(i):
        group = pl.ds(i * per_chunk, per_chunk)
        return pltpu.make_async_copy(weights.at[0, 0, group], wbuf.at[group], w_sem.at[i])

    @pl.when(sec == 0)
    def _():
        for copy in small:
            copy.start()
        for i in range(CHUNKS):
            load_weights(i).start()

    mask_copy.wait()

    def store(h, f, i):
        part = final.at[0, f, :, pl.ds(h * half, half), pl.ds(i * LANES, LANES)]
        return pltpu.make_async_copy(out.at[h, f, i], part, out_sem.at[h, f, i])

    stores = [store(h, f, i) for h in range(rows // half) for f in range(3) for i in range(tiles)]
    for k in range(parts):
        for copy in loads[k]:
            copy.wait()
        for x in range(4 * k, 4 * k + 4):
            h = x // half
            w = mask[0, x : x + 1, :].astype(F32)
            here = p[x + 1]
            span = here.shape[1]
            plus = pltpu.roll(here, span - 1, 1)[:, :width]
            minus = pltpu.roll(here, 1, 1)[:, :width]
            gradient = p[x + 2, :, :width] - p[x, :, :width]
            values = (
                here[:, :width],
                w * (u[x] - 0.5 * gradient),
                w * (v[x] - 0.5 * (plus - minus)),
            )
            for f, value in enumerate(values):
                for i in range(tiles):
                    flat = out.at[h, f, i].reshape(levels * half, LANES)
                    at = pl.ds(x % half, levels, stride=half)
                    flat[at, :] = value[:, i * LANES : (i + 1) * LANES]
        if (4 * k + 4) % half == 0:
            per_half = 3 * tiles
            h = (4 * k + 4) // half - 1
            for copy in stores[h * per_half : (h + 1) * per_half]:
                copy.start()

    @pl.when(sec == 0)
    def _():
        for copy in small:
            copy.wait()
        in_per_row, out_per_row = width // in_width, width // out_width
        in_blocks, out_blocks = rows * in_per_row, rows * out_per_row
        slots = returned.shape[0] * out_blocks
        slot_col = upright(wide_row(tile_in) * out_blocks + wide_row(target_in))
        slot = slot_key(iota((pairs, slots), 1), out_blocks, rows, out_per_row)
        picking = (slot == slot_col).astype(F32).astype(BF16)
        per_pair = dot(picking, returned[...].reshape(slots, out_width))
        key = block_key(iota((in_blocks, pairs), 0), rows, in_per_row).astype(F32)
        owner = (key == wide_row(source_in)).astype(F32)
        total = jnp.zeros((in_blocks, in_width), F32)
        for j in range(0, pairs, 2):
            if j % per_chunk == 0:
                load_weights(j // per_chunk).wait()
            left = jnp.concatenate(
                [owner[:, i : i + 1] * per_pair[i : i + 1] for i in (j, j + 1)], axis=1
            ).astype(BF16)
            total = total + lax.dot_general(
                left, wide(wbuf, j), (((1,), (1,)), ((), ())), preferred_element_type=F32
            )
        sbuf[...] = jnp.concatenate(
            [total[i * rows : (i + 1) * rows] for i in range(in_per_row)], axis=1
        )
        surface_copy = pltpu.make_async_copy(sbuf, surface.at[0], small_sem.at[1])
        surface_copy.start()
        surface_copy.wait()

    @pl.when(sec == 1)
    def _():
        surface_copy = pltpu.make_async_copy(surface_in, surface, small_sem.at[1])
        surface_copy.start()
        surface_copy.wait()

    for copy in stores:
        copy.wait()


def local(n_gx, n_gy, *args):
    state, speed, mask, vertical, temp, coef, gain, tile, source, target, weights = args
    coef = coef.T
    gain = gain.reshape(1, -1)
    tile = tile.reshape(source.shape)
    _, fields, levels, rows, width = state.shape
    pairs, in_width, out_width = weights.shape[2:]
    out_blocks = rows * width // out_width
    hbm = pl.BlockSpec(memory_space=pltpu.HBM)
    free = pl.BlockSpec(memory_space=pl.ANY)
    dma = pltpu.SemaphoreType.DMA
    tiled = pltpu.VMEM((fields, width // LANES, levels, rows, LANES), F32)
    span = width + LANES
    tall = pltpu.VMEM((rows + 2, levels, span), F32)
    ext = pltpu.VMEM((rows, levels, LANES), F32)
    params = dict(has_side_effects=True, vmem_limit_bytes=62 * 2**20)
    p2, u1, v1, surface, returned = pl.pallas_call(
        functools.partial(kernel, n_gx, n_gy),
        out_shape=(
            jax.ShapeDtypeStruct((rows + 2, levels, span), F32),
            jax.ShapeDtypeStruct((rows, levels, width), F32),
            jax.ShapeDtypeStruct((rows, levels, width), F32),
            jax.ShapeDtypeStruct(temp.shape, F32),
            jax.ShapeDtypeStruct((n_gx, out_blocks, out_width), BF16),
        ),
        in_specs=[hbm] * 11,
        out_specs=(free,) * 5,
        scratch_shapes=[
            pltpu.VMEM(speed.shape, F32),
            pltpu.VMEM(mask.shape, jnp.int32),
            pltpu.VMEM(vertical.shape, F32),
            pltpu.VMEM(temp.shape, F32),
            pltpu.VMEM(coef.shape, F32),
            pltpu.VMEM(gain.shape, F32),
            pltpu.VMEM(tile.shape, jnp.int32),
            pltpu.VMEM(source.shape, jnp.int32),
            pltpu.VMEM(target.shape, jnp.int32),
            tiled,
            pltpu.VMEM((pairs, in_width, out_width), BF16),
            tall,
            tall,
            tall,
            pltpu.VMEM((rows, levels, span), F32),
            tall,
            ext,
            ext,
            pltpu.VMEM((rows, span), F32),
            pltpu.VMEM((rows, span), F32),
            pltpu.VMEM((STAGES, 2, levels, span), BF16),
            pltpu.VMEM((STAGES, 2, levels, span), BF16),
            pltpu.VMEM((fields, 2, levels, LANES), F32),
            pltpu.VMEM((3, 2, levels, LANES), F32),
            pltpu.VMEM((2, levels, LANES), F32),
            pltpu.VMEM((2, levels, LANES), F32),
            pltpu.VMEM((2, rows, LANES), F32),
            pltpu.VMEM((2, rows, LANES), jnp.int32),
            pltpu.VMEM((n_gx, out_blocks, out_width), BF16),
            pltpu.VMEM((n_gx, out_blocks, out_width), BF16),
            pltpu.VMEM((out_blocks, out_width), BF16),
            pltpu.VMEM((n_gx, out_blocks, out_width), BF16),
            pltpu.VMEM((rows, width), F32),
            dma((fields, width // LANES)),
            dma((9,)),
            dma(()),
            dma((CHUNKS,)),
            dma((STAGES, 2)),
            dma((STAGES, 2)),
            dma((7, 2)),
            dma((7, 2)),
            dma((n_gx,)),
            dma((n_gx,)),
            dma((n_gx,)),
            dma((n_gx,)),
            dma((5,)),
        ],
        compiler_params=pltpu.CompilerParams(collective_id=0, **params),
    )(state, speed, mask, vertical, temp, coef, gain, tile, source, target, weights)
    return pl.pallas_call(
        last_kernel,
        out_shape=(
            jax.ShapeDtypeStruct(state.shape, F32),
            jax.ShapeDtypeStruct(temp.shape, F32),
        ),
        in_specs=[hbm] * 10,
        out_specs=(free, free),
        scratch_shapes=[
            tall,
            pltpu.VMEM((rows, levels, width), F32),
            pltpu.VMEM((rows, levels, width), F32),
            pltpu.VMEM(mask.shape, jnp.int32),
            pltpu.VMEM(returned.shape, BF16),
            pltpu.VMEM(tile.shape, jnp.int32),
            pltpu.VMEM(source.shape, jnp.int32),
            pltpu.VMEM(target.shape, jnp.int32),
            pltpu.VMEM((pairs, in_width, out_width), BF16),
            pltpu.VMEM((rows, width), F32),
            pltpu.VMEM((rows // 8, fields, width // LANES, levels, 8, LANES), F32),
            dma((rows // 4, 3)),
            dma((rows // 8, fields, width // LANES)),
            dma((6,)),
            dma((CHUNKS,)),
        ],
        compiler_params=pltpu.CompilerParams(**params),
    )(p2, u1, v1, mask, surface, returned, tile, source, target, weights)


def solution(mesh):
    return jax.shard_map(
        functools.partial(local, mesh.shape["gx"], mesh.shape["gy"]),
        mesh=mesh,
        in_specs=(
            P("sec", None, None, "gx", "gy"),
            P("sec", "gx", "gy"),
            P("sec", "gx", "gy"),
            P("sec", None, None),
            P("sec", "gx", "gy"),
            P(),
            P(),
            P("gx", "gy", None, None),
            P("gx", "gy", None),
            P("gx", "gy", None),
            P("gx", "gy", None, None, None),
        ),
        out_specs=(P("sec", None, None, "gx", "gy"), P("sec", "gx", "gy")),
        check_vma=False,
    )
```

```python
import functools

import jax
import jax.numpy as jnp
from jax import lax
from jax.experimental import pallas as pl
from jax.experimental.pallas import tpu as pltpu
from jax.sharding import PartitionSpec as P

MESH = pl.DeviceIdType.MESH
F32 = jnp.float32
BF16 = jnp.bfloat16
LANES = 128
CHUNKS = 8
EXCHANGES = 2
MARGIN = 4
P_FIELD, U_FIELD, V_FIELD = 0, 1, 2
SPEED, MASK, P_COLS, V_COLS, U_COLS = range(5)


def iota(shape, axis):
    return lax.broadcasted_iota(jnp.int32, shape, axis)


def split(value, parts):
    pieces = []
    for _ in range(parts):
        piece = value.astype(BF16)
        pieces.append(piece)
        value = value - piece.astype(F32)
    return pieces


def dot(a, b):
    return jnp.dot(a, b, preferred_element_type=F32)


def block_key(index, rows, per_row):
    return (index & (rows - 1)) * per_row + (index >> (rows.bit_length() - 1))


def wide_row(ref):
    return ref[0, 0].reshape(1, ref.shape[-1]).astype(F32)


def upright(row):
    size = row.shape[1]
    diagonal = iota((size, size), 0) == iota((size, size), 1)
    return jnp.sum(jnp.where(diagonal, row, 0.0), axis=1, keepdims=True)


def slot_key(index, blocks, rows, per_row):
    within = block_key(index & (blocks - 1), rows, per_row)
    return ((index >> (blocks.bit_length() - 1)) * blocks + within).astype(F32)


def wide(weights, j):
    return jnp.concatenate([weights[j], weights[j + 1]], axis=1)


def kernel(
    n_gx,
    n_gy,
    state,
    speed_in,
    mask_in,
    vertical_in,
    temp_in,
    coef_in,
    gain_in,
    tile_hbm,
    source_hbm,
    target_hbm,
    weights,
    p2_out,
    u1_out,
    v1_out,
    surface,
    returned,
    speed,
    mask,
    vertical,
    temp,
    coef,
    gain,
    tile_in,
    source_in,
    target_in,
    raw,
    wbuf,
    u0,
    p1,
    u1,
    v1,
    p2,
    p_ext,
    v_ext,
    c_wide,
    w_wide,
    rowsend,
    rowrecv,
    colsend,
    u_recv,
    v_recv,
    p_recv,
    speed_recv,
    mask_recv,
    ybuf,
    yrecv,
    tsend,
    trecv,
    sbuf,
    load_sem,
    small_sem,
    surface_sem,
    w_sem,
    row_send,
    row_recv,
    col_send,
    col_recv,
    y_send,
    y_recv,
    t_send,
    t_recv,
    out_sem,
):
    sec = lax.axis_index("sec")
    a = lax.axis_index("gx")
    b = lax.axis_index("gy")
    levels, rows, width = state.shape[2:]
    tiles = width // LANES
    pairs, in_width, out_width = wbuf.shape
    in_per_row = width // in_width
    out_per_row = width // out_width
    in_blocks = rows * in_per_row
    out_blocks = rows * out_per_row
    per_chunk = pairs // CHUNKS

    def load(f, i):
        part = state.at[0, f, :, :, pl.ds(i * LANES, LANES)]
        return pltpu.make_async_copy(part, raw.at[f, i], load_sem.at[f, i])

    def load_weights(i):
        part = pl.ds(i * per_chunk, per_chunk)
        return pltpu.make_async_copy(weights.at[0, 0, part], wbuf.at[part], w_sem.at[i])

    small = [
        pltpu.make_async_copy(src, dst, small_sem.at[i])
        for i, (src, dst) in enumerate(
            (
                (speed_in, speed),
                (mask_in, mask),
                (vertical_in, vertical),
                (temp_in, temp),
                (coef_in, coef),
                (gain_in, gain),
                (tile_hbm, tile_in),
                (source_hbm, source_in),
                (target_hbm, target_in),
            )
        )
    ]
    for f in (1, 2):
        for i in range(tiles):
            load(f, i).start()
    for copy in small:
        copy.start()
    for i in range(tiles):
        load(0, i).start()

    @pl.when(sec == 0)
    def _():
        for i in range(CHUNKS):
            load_weights(i).start()

    barrier = pltpu.get_barrier_semaphore()
    for s in range(2):
        for t in range(n_gx):

            @pl.when(jnp.logical_or(s != sec, t != a))
            def _():
                pl.semaphore_signal(barrier, inc=1, device_id=(s, t, b), device_id_type=MESH)

    row_ok = (a > 0, a < n_gx - 1)
    col_ok = (b > 0, b < n_gy - 1)

    for side in range(2):

        @pl.when(col_ok[side])
        def _(side=side):
            pl.semaphore_signal(
                barrier, inc=1, device_id=(sec, a, b + 2 * side - 1), device_id_type=MESH
            )

    beside = (b > 0).astype(jnp.int32) + (b < n_gy - 1).astype(jnp.int32)

    for side in range(2):

        @pl.when(jnp.logical_not(row_ok[side]))
        def _(side=side):
            for buf in (u0, p1, u1, p2):
                buf[side * (rows + 1)] = jnp.zeros(buf.shape[1:], F32)

        @pl.when(jnp.logical_not(col_ok[side]))
        def _(side=side):
            u_recv[side] = jnp.zeros((levels, LANES), F32)
            v_recv[side] = jnp.zeros((levels, LANES), F32)
            p_recv[side] = jnp.zeros((levels, LANES), F32)
            speed_recv[side] = jnp.zeros((rows, LANES), F32)
            mask_recv[side] = jnp.zeros((rows, LANES), jnp.int32)

    def row_copy(exchange, side):
        part = pl.ds(0, 2 * levels if exchange else rowsend.shape[2])
        return pltpu.make_async_remote_copy(
            src_ref=rowsend.at[exchange, side, part],
            dst_ref=rowrecv.at[exchange, 1 - side, part],
            send_sem=row_send.at[exchange, side],
            recv_sem=row_recv.at[exchange, side],
            device_id=(sec, a - 1 if side == 0 else a + 1, b),
            device_id_type=MESH,
        )

    def col_copy(kind, side):
        edge = pl.ds(0 if side == 0 else width - LANES, LANES)
        other = 1 - side
        src, dst = {
            SPEED: (speed.at[0, :, edge], speed_recv.at[other]),
            MASK: (mask.at[0, :, edge], mask_recv.at[other]),
            P_COLS: (colsend.at[P_FIELD, side], p_recv.at[other]),
            V_COLS: (colsend.at[V_FIELD, side], v_recv.at[other]),
            U_COLS: (colsend.at[U_FIELD, side], u_recv.at[other]),
        }[kind]
        return pltpu.make_async_remote_copy(
            src_ref=src,
            dst_ref=dst,
            send_sem=col_send.at[kind, side],
            recv_sem=col_recv.at[kind, side],
            device_id=(sec, a, b - 1 if side == 0 else b + 1),
            device_id_type=MESH,
        )

    def send_cols(*kinds):
        for kind in kinds:
            for side in range(2):

                @pl.when(col_ok[side])
                def _(side=side, kind=kind):
                    col_copy(kind, side).start()

    def wait_cols():
        for kind in range(5):
            for side in range(2):

                @pl.when(col_ok[side])
                def _(side=side, kind=kind):
                    col_copy(kind, 1 - side).wait_recv()

    def wait_sent():
        for side in range(2):
            for kind in range(5):

                @pl.when(col_ok[side])
                def _(side=side, kind=kind):
                    col_copy(kind, side).wait_send()

            for exchange in range(EXCHANGES):

                @pl.when(row_ok[side])
                def _(side=side, exchange=exchange):
                    row_copy(exchange, side).wait_send()

    def send_edges(exchange, u_buf, p_row, v_row):
        for side in range(2):

            @pl.when(row_ok[side])
            def _(side=side):
                x = side * (rows - 1)
                inner = -u_buf[x] if side else u_buf[x + 2]
                c = c_wide[x : x + 1, :]
                partial = p_row(x) - c * (inner + along_y(v_row(x)))
                rowsend[exchange, side, :levels] = u_buf[x + 1].astype(BF16)
                rowsend[exchange, side, levels : 2 * levels] = partial.astype(BF16)
                if exchange == 0:
                    high, low = [piece.astype(F32) for piece in split(c, 2)]
                    at = iota((rowsend.shape[2] - 2 * levels, c.shape[1]), 0)
                    both = jnp.where(at == 0, high, jnp.where(at == 1, low, 0.0))
                    rowsend[exchange, side, 2 * levels :] = both.astype(BF16)
                row_copy(exchange, side).start()

    def wait_edges(exchange, u_buf, p_buf):
        for side in range(2):

            @pl.when(row_ok[side])
            def _(side=side):
                row_copy(exchange, 1 - side).wait_recv()
                at = rows + 1 if side else 0
                u_buf[at] = rowrecv[exchange, side, :levels].astype(F32)
                partial = rowrecv[exchange, side, levels : 2 * levels].astype(F32)
                c = rowrecv[0, side, 2 * levels :].astype(F32)
                term = (c[0:1] + c[1:2]) * u_buf[rows if side else 1]
                p_buf[at] = mix(partial + term if side else partial - term)

    lane = iota((levels, LANES), 1)

    def flat(buf, f):
        return [buf.at[f, i].reshape(levels * rows, LANES) for i in range(tiles)]

    flat_raw = [flat(raw, f) for f in range(3)]

    def column(f, x):
        parts = [ref[pl.ds(x, levels, stride=rows), :] for ref in flat_raw[f]]
        return jnp.concatenate(parts, axis=1)

    def edges(f, x):
        return [flat_raw[f][i][pl.ds(x, levels, stride=rows), :] for i in (0, tiles - 1)]

    def loaded(f):
        for i in range(tiles):
            load(f, i).wait()

    mine = lane // MARGIN

    def pack(f, x, carry):
        low, high = carry
        first, last = edges(f, x)
        low = jnp.where(mine == x, pltpu.roll(first, MARGIN * x, 1), low)
        high = jnp.where(mine == x, pltpu.roll(last, MARGIN * x + MARGIN, 1), high)
        return low, high

    def pack_all(f):
        blank = jnp.zeros((levels, LANES), F32)

        def several(i, carry):
            for k in range(4):
                carry = pack(f, 4 * i + k, carry)
            return carry

        low, high = lax.fori_loop(0, rows // 4, several, (blank, blank))
        colsend[f, 0] = low
        colsend[f, 1] = high

    def margin(ref, x):
        before = pltpu.roll(ref[0], LANES - MARGIN - MARGIN * x, 1)
        after = pltpu.roll(ref[1], lax.rem(LANES - MARGIN * x, LANES), 1)
        rest = jnp.where(lane >= LANES - MARGIN, before, 0.0)
        return jnp.where(lane < MARGIN, after, rest)

    def along_y(value):
        return pltpu.roll(value, value.shape[1] - 1, 1) - pltpu.roll(value, 1, 1)

    def mix(right_side):
        high, low = split(right_side, 2)
        return right_side + dot(mixer, jnp.concatenate([high, low, high, low], axis=0))

    def pressure_row(x, p, u_buf, v):
        divergence = (u_buf[x + 2] - u_buf[x]) + along_y(v)
        return mix(p - c_wide[pl.ds(x, 1), :] * divergence)

    def sweep(row, first, count):
        step = next(k for k in (8, 7, 6, 5, 4, 3, 2, 1) if count % k == 0)

        def several(i, c):
            for k in range(step):
                row(first + i * step + k)
            return c

        lax.fori_loop(0, count // step, several, 0)

    loaded(U_FIELD)
    pack_all(U_FIELD)
    pl.semaphore_wait(barrier, 2 * n_gx - 1 + beside)
    send_cols(U_COLS)
    loaded(V_FIELD)
    pack_all(V_FIELD)
    send_cols(V_COLS)
    for copy in small:
        copy.wait()
    send_cols(SPEED, MASK)
    loaded(P_FIELD)
    pack_all(P_FIELD)
    send_cols(P_COLS)
    m_high, m_low = split(vertical[0], 2)
    m_high, m_low = m_high.astype(F32), m_low.astype(F32)
    mixer = jnp.concatenate([m_high, m_high, m_low, m_low], axis=1).astype(BF16)

    slots = n_gx * out_blocks
    slot_row = wide_row(tile_in) * out_blocks + wide_row(target_in)

    def y_copy(t):
        return pltpu.make_async_remote_copy(
            src_ref=ybuf.at[t],
            dst_ref=yrecv.at[a],
            send_sem=y_send.at[t],
            recv_sem=y_recv.at[a],
            device_id=(1, t, b),
            device_id_type=MESH,
        )

    def t_copy(t):
        return pltpu.make_async_remote_copy(
            src_ref=tsend,
            dst_ref=trecv.at[a],
            send_sem=t_send.at[t],
            recv_sem=t_recv.at[a],
            device_id=(0, t, b),
            device_id_type=MESH,
        )

    @pl.when(sec == 0)
    def _():
        drivers = [
            jnp.concatenate([raw[f, i, 0] for i in range(tiles)], axis=1) for f in range(3)
        ] + [temp[0]]
        heat = jnp.zeros((rows, width), F32)
        factors, gains = coef[...], gain[...]
        for f in range(factors.shape[1]):
            total = factors[0:1, f : f + 1] * drivers[0]
            for k in range(1, 4):
                total = total + factors[k : k + 1, f : f + 1] * drivers[k]
            heat = heat + gains[:, f : f + 1] * jnp.tanh(total).astype(BF16).astype(F32)
        blocks = jnp.concatenate(
            [heat[:, i * in_width : (i + 1) * in_width] for i in range(in_per_row)], axis=0
        )
        source_col = upright(wide_row(source_in))
        key = block_key(iota((pairs, in_blocks), 1), rows, in_per_row).astype(F32)
        picking = (source_col == key).astype(F32).astype(BF16)
        high, low = [dot(picking, piece) for piece in split(blocks, 2)]
        sub = iota((8, out_width), 0)
        groups = []
        for g in range(pairs // 8):
            if g % (per_chunk // 8) == 0:
                load_weights(g * 8 // per_chunk).wait()
            part = slice(8 * g, 8 * g + 8)
            left = jnp.concatenate([high[part], low[part]], axis=0).astype(BF16)
            group = jnp.zeros((8, out_width), F32)
            for i in range(0, 8, 2):
                both = dot(left, wide(wbuf, 8 * g + i))
                both = both[:8] + both[8:]
                group = jnp.where(sub == i, both[:, :out_width], group)
                group = jnp.where(sub == i + 1, both[:, out_width:], group)
            groups.append(group)
        heated = jnp.concatenate(groups, axis=0)
        placing = (slot_key(iota((slots, pairs), 0), out_blocks, rows, out_per_row) == slot_row).astype(F32).astype(BF16)
        dense = sum(dot(placing, piece) for piece in split(heated, 3))
        ybuf[...] = dense.astype(BF16).reshape(n_gx, out_blocks, out_width)
        for t in range(n_gx):
            y_copy(t).start()

    def fill(x):
        u0[x + 1, :, :width] = column(U_FIELD, x)

    sweep(fill, 0, rows)
    wait_cols()

    def fill_margins(x):
        u0[x + 1, :, width:] = margin(u_recv, x)
        v_ext[x] = margin(v_recv, x)
        p_ext[x] = margin(p_recv, x)

    sweep(fill_margins, 0, rows)
    across = iota((rows, LANES), 1)

    def around(pair):
        rest = jnp.where(across >= LANES - MARGIN, pair[0], 0.0)
        return jnp.where(across < MARGIN, pair[1], rest)

    c_wide[:, :width] = speed[0]
    c_wide[:, width:] = around(speed_recv[...])
    w_wide[:, :width] = mask[0].astype(F32)
    w_wide[:, width:] = around(mask_recv[...].astype(F32))

    def wide_column(f, ext, x):
        return jnp.concatenate([column(f, x), ext[x]], axis=1)

    def p_first(x):
        return wide_column(P_FIELD, p_ext, x)

    def v_first(x):
        return wide_column(V_FIELD, v_ext, x)

    def first_pressure(x):
        p1[x + 1] = pressure_row(x, p_first(x), u0, v_first(x))

    send_edges(0, u0, p_first, v_first)
    sweep(first_pressure, 1, rows - 2)
    wait_edges(0, u0, p1)
    first_pressure(0)
    first_pressure(rows - 1)

    def first_velocity(x):
        w = w_wide[pl.ds(x, 1), :]
        u1[x + 1] = w * (u0[x + 1] - 0.5 * (p1[x + 2] - p1[x]))
        v1[x] = w * (v_first(x) - 0.5 * along_y(p1[x + 1]))

    for x in (0, 1, rows - 2, rows - 1):
        first_velocity(x)
    send_edges(1, u1, lambda x: p1[x + 1], lambda x: v1[x])
    sweep(first_velocity, 2, rows - 4)

    near = pl.ds(0, width)
    stores = [
        pltpu.make_async_copy(u1.at[pl.ds(1, rows), :, near], u1_out, out_sem.at[0]),
        pltpu.make_async_copy(v1.at[:, :, near], v1_out, out_sem.at[1]),
    ]
    for i, (first, count) in enumerate(((2, rows - 2), (0, 2), (rows, 2))):
        part = pl.ds(first, count)
        stores.append(pltpu.make_async_copy(p2.at[part], p2_out.at[part], out_sem.at[2 + i]))
    stores[0].start()
    stores[1].start()

    def as_blocks(value):
        return jnp.concatenate(
            [value[:, i * out_width : (i + 1) * out_width] for i in range(out_per_row)], axis=0
        )

    @pl.when(sec == 1)
    def _():
        heating = jnp.zeros((out_blocks, out_width), F32)
        for t in range(n_gx):
            pltpu.make_async_remote_copy(
                src_ref=ybuf.at[t],
                dst_ref=yrecv.at[t],
                send_sem=y_send.at[t],
                recv_sem=y_recv.at[t],
                device_id=(0, t, b),
                device_id_type=MESH,
            ).wait_recv()
            heating = heating + yrecv[t].astype(F32)
        ocean = as_blocks(temp[0]) + as_blocks(mask[0].astype(F32)) * heating
        tsend[...] = ocean.astype(BF16)
        for t in range(n_gx):
            t_copy(t).start()

        sbuf[...] = jnp.concatenate(
            [ocean[i * rows : (i + 1) * rows] for i in range(out_per_row)], axis=1
        )

    def second_pressure(x):
        p2[x + 1] = pressure_row(x, p1[x + 1], u1, v1[x])

    sweep(second_pressure, 1, rows - 2)
    stores[2].start()
    wait_edges(1, u1, p2)
    second_pressure(0)
    second_pressure(rows - 1)
    stores[3].start()
    stores[4].start()
    wait_sent()

    @pl.when(sec == 0)
    def _():
        for t in range(n_gx):
            y_copy(t).wait_send()
        for t in range(n_gx):
            pltpu.make_async_remote_copy(
                src_ref=tsend,
                dst_ref=trecv.at[t],
                send_sem=t_send.at[t],
                recv_sem=t_recv.at[t],
                device_id=(1, t, b),
                device_id_type=MESH,
            ).wait_recv()
        returned_copy = pltpu.make_async_copy(trecv, returned, surface_sem)
        returned_copy.start()
        returned_copy.wait()

    @pl.when(sec == 1)
    def _():
        surface_copy = pltpu.make_async_copy(sbuf, surface.at[0], surface_sem)
        surface_copy.start()
        for t in range(n_gx):
            t_copy(t).wait_send()
        surface_copy.wait()

    for copy in stores:
        copy.wait()


def last_kernel(
    p_in,
    u_in,
    v_in,
    mask_in,
    surface_in,
    returned_in,
    tile_hbm,
    source_hbm,
    target_hbm,
    weights,
    final,
    surface,
    p,
    u,
    v,
    mask,
    returned,
    tile_in,
    source_in,
    target_in,
    wbuf,
    sbuf,
    out,
    sem,
    out_sem,
    small_sem,
    w_sem,
):
    sec = lax.axis_index("sec")
    rows, levels, width = u_in.shape
    tiles = width // LANES
    parts = rows // 4
    half = 8

    mask_copy = pltpu.make_async_copy(mask_in, mask, small_sem.at[0])
    mask_copy.start()
    loads = []
    for k in range(parts):
        first = 0 if k == 0 else 4 * k + 2
        p_rows = pl.ds(first, 4 * k + 6 - first)
        part = pl.ds(4 * k, 4)
        loads.append(
            [
                pltpu.make_async_copy(src, dst, sem.at[k, i])
                for i, (src, dst) in enumerate(
                    (
                        (p_in.at[p_rows], p.at[p_rows]),
                        (u_in.at[part], u.at[part]),
                        (v_in.at[part], v.at[part]),
                    )
                )
            ]
        )
        for copy in loads[-1]:
            copy.start()
    small = [
        pltpu.make_async_copy(src, dst, small_sem.at[2 + i])
        for i, (src, dst) in enumerate(
            (
                (returned_in, returned),
                (tile_hbm, tile_in),
                (source_hbm, source_in),
                (target_hbm, target_in),
            )
        )
    ]
    pairs, in_width, out_width = wbuf.shape
    per_chunk = pairs // CHUNKS

    def load_weights(i):
        group = pl.ds(i * per_chunk, per_chunk)
        return pltpu.make_async_copy(weights.at[0, 0, group], wbuf.at[group], w_sem.at[i])

    @pl.when(sec == 0)
    def _():
        for copy in small:
            copy.start()
        for i in range(CHUNKS):
            load_weights(i).start()

    mask_copy.wait()

    def store(h, f, i):
        part = final.at[0, f, :, pl.ds(h * half, half), pl.ds(i * LANES, LANES)]
        return pltpu.make_async_copy(out.at[h, f, i], part, out_sem.at[h, f, i])

    stores = [store(h, f, i) for h in range(rows // half) for f in range(3) for i in range(tiles)]
    for k in range(parts):
        for copy in loads[k]:
            copy.wait()
        for x in range(4 * k, 4 * k + 4):
            h = x // half
            w = mask[0, x : x + 1, :].astype(F32)
            here = p[x + 1]
            span = here.shape[1]
            plus = pltpu.roll(here, span - 1, 1)[:, :width]
            minus = pltpu.roll(here, 1, 1)[:, :width]
            gradient = p[x + 2, :, :width] - p[x, :, :width]
            values = (
                here[:, :width],
                w * (u[x] - 0.5 * gradient),
                w * (v[x] - 0.5 * (plus - minus)),
            )
            for f, value in enumerate(values):
                for i in range(tiles):
                    flat = out.at[h, f, i].reshape(levels * half, LANES)
                    at = pl.ds(x % half, levels, stride=half)
                    flat[at, :] = value[:, i * LANES : (i + 1) * LANES]
        if (4 * k + 4) % half == 0:
            per_half = 3 * tiles
            h = (4 * k + 4) // half - 1
            for copy in stores[h * per_half : (h + 1) * per_half]:
                copy.start()

    @pl.when(sec == 0)
    def _():
        for copy in small:
            copy.wait()
        in_per_row, out_per_row = width // in_width, width // out_width
        in_blocks, out_blocks = rows * in_per_row, rows * out_per_row
        slots = returned.shape[0] * out_blocks
        slot_col = upright(wide_row(tile_in) * out_blocks + wide_row(target_in))
        slot = slot_key(iota((pairs, slots), 1), out_blocks, rows, out_per_row)
        picking = (slot == slot_col).astype(F32).astype(BF16)
        per_pair = dot(picking, returned[...].reshape(slots, out_width))
        key = block_key(iota((in_blocks, pairs), 0), rows, in_per_row).astype(F32)
        owner = (key == wide_row(source_in)).astype(F32)
        total = jnp.zeros((in_blocks, in_width), F32)
        for j in range(0, pairs, 2):
            if j % per_chunk == 0:
                load_weights(j // per_chunk).wait()
            left = jnp.concatenate(
                [owner[:, i : i + 1] * per_pair[i : i + 1] for i in (j, j + 1)], axis=1
            ).astype(BF16)
            total = total + lax.dot_general(
                left, wide(wbuf, j), (((1,), (1,)), ((), ())), preferred_element_type=F32
            )
        sbuf[...] = jnp.concatenate(
            [total[i * rows : (i + 1) * rows] for i in range(in_per_row)], axis=1
        )
        surface_copy = pltpu.make_async_copy(sbuf, surface.at[0], small_sem.at[1])
        surface_copy.start()
        surface_copy.wait()

    @pl.when(sec == 1)
    def _():
        surface_copy = pltpu.make_async_copy(surface_in, surface, small_sem.at[1])
        surface_copy.start()
        surface_copy.wait()

    for copy in stores:
        copy.wait()


def local(n_gx, n_gy, *args):
    state, speed, mask, vertical, temp, coef, gain, tile, source, target, weights = args
    coef = coef.T
    gain = gain.reshape(1, -1)
    tile = tile.reshape(source.shape)
    _, fields, levels, rows, width = state.shape
    pairs, in_width, out_width = weights.shape[2:]
    out_blocks = rows * width // out_width
    hbm = pl.BlockSpec(memory_space=pltpu.HBM)
    free = pl.BlockSpec(memory_space=pl.ANY)
    dma = pltpu.SemaphoreType.DMA
    tiled = pltpu.VMEM((fields, width // LANES, levels, rows, LANES), F32)
    span = width + LANES
    tall = pltpu.VMEM((rows + 2, levels, span), F32)
    ext = pltpu.VMEM((rows, levels, LANES), F32)
    params = dict(has_side_effects=True, vmem_limit_bytes=62 * 2**20)
    p2, u1, v1, surface, returned = pl.pallas_call(
        functools.partial(kernel, n_gx, n_gy),
        out_shape=(
            jax.ShapeDtypeStruct((rows + 2, levels, span), F32),
            jax.ShapeDtypeStruct((rows, levels, width), F32),
            jax.ShapeDtypeStruct((rows, levels, width), F32),
            jax.ShapeDtypeStruct(temp.shape, F32),
            jax.ShapeDtypeStruct((n_gx, out_blocks, out_width), BF16),
        ),
        in_specs=[hbm] * 11,
        out_specs=(free,) * 5,
        scratch_shapes=[
            pltpu.VMEM(speed.shape, F32),
            pltpu.VMEM(mask.shape, jnp.int32),
            pltpu.VMEM(vertical.shape, F32),
            pltpu.VMEM(temp.shape, F32),
            pltpu.VMEM(coef.shape, F32),
            pltpu.VMEM(gain.shape, F32),
            pltpu.VMEM(tile.shape, jnp.int32),
            pltpu.VMEM(source.shape, jnp.int32),
            pltpu.VMEM(target.shape, jnp.int32),
            tiled,
            pltpu.VMEM((pairs, in_width, out_width), BF16),
            tall,
            tall,
            tall,
            pltpu.VMEM((rows, levels, span), F32),
            tall,
            ext,
            ext,
            pltpu.VMEM((rows, span), F32),
            pltpu.VMEM((rows, span), F32),
            pltpu.VMEM((EXCHANGES, 2, 2 * levels + 16, span), BF16),
            pltpu.VMEM((EXCHANGES, 2, 2 * levels + 16, span), BF16),
            pltpu.VMEM((fields, 2, levels, LANES), F32),
            pltpu.VMEM((2, levels, LANES), F32),
            pltpu.VMEM((2, levels, LANES), F32),
            pltpu.VMEM((2, levels, LANES), F32),
            pltpu.VMEM((2, rows, LANES), F32),
            pltpu.VMEM((2, rows, LANES), jnp.int32),
            pltpu.VMEM((n_gx, out_blocks, out_width), BF16),
            pltpu.VMEM((n_gx, out_blocks, out_width), BF16),
            pltpu.VMEM((out_blocks, out_width), BF16),
            pltpu.VMEM((n_gx, out_blocks, out_width), BF16),
            pltpu.VMEM((rows, width), F32),
            dma((fields, width // LANES)),
            dma((9,)),
            dma(()),
            dma((CHUNKS,)),
            dma((EXCHANGES, 2)),
            dma((EXCHANGES, 2)),
            dma((5, 2)),
            dma((5, 2)),
            dma((n_gx,)),
            dma((n_gx,)),
            dma((n_gx,)),
            dma((n_gx,)),
            dma((5,)),
        ],
        compiler_params=pltpu.CompilerParams(collective_id=0, **params),
    )(state, speed, mask, vertical, temp, coef, gain, tile, source, target, weights)
    return pl.pallas_call(
        last_kernel,
        out_shape=(
            jax.ShapeDtypeStruct(state.shape, F32),
            jax.ShapeDtypeStruct(temp.shape, F32),
        ),
        in_specs=[hbm] * 10,
        out_specs=(free, free),
        scratch_shapes=[
            tall,
            pltpu.VMEM((rows, levels, width), F32),
            pltpu.VMEM((rows, levels, width), F32),
            pltpu.VMEM(mask.shape, jnp.int32),
            pltpu.VMEM(returned.shape, BF16),
            pltpu.VMEM(tile.shape, jnp.int32),
            pltpu.VMEM(source.shape, jnp.int32),
            pltpu.VMEM(target.shape, jnp.int32),
            pltpu.VMEM((pairs, in_width, out_width), BF16),
            pltpu.VMEM((rows, width), F32),
            pltpu.VMEM((rows // 8, fields, width // LANES, levels, 8, LANES), F32),
            dma((rows // 4, 3)),
            dma((rows // 8, fields, width // LANES)),
            dma((6,)),
            dma((CHUNKS,)),
        ],
        compiler_params=pltpu.CompilerParams(**params),
    )(p2, u1, v1, mask, surface, returned, tile, source, target, weights)


def solution(mesh):
    return jax.shard_map(
        functools.partial(local, mesh.shape["gx"], mesh.shape["gy"]),
        mesh=mesh,
        in_specs=(
            P("sec", None, None, "gx", "gy"),
            P("sec", "gx", "gy"),
            P("sec", "gx", "gy"),
            P("sec", None, None),
            P("sec", "gx", "gy"),
            P(),
            P(),
            P("gx", "gy", None, None),
            P("gx", "gy", None),
            P("gx", "gy", None),
            P("gx", "gy", None, None, None),
        ),
        out_specs=(P("sec", None, None, "gx", "gy"), P("sec", "gx", "gy")),
        check_vma=False,
    )
```

```python
import functools

import jax
import jax.numpy as jnp
from jax import lax
from jax.experimental import pallas as pl
from jax.experimental.pallas import tpu as pltpu
from jax.sharding import PartitionSpec as P

MESH = pl.DeviceIdType.MESH
F32 = jnp.float32
BF16 = jnp.bfloat16
LANES = 128
CHUNKS = 8
EXCHANGES = 2
MARGIN = 4
P_FIELD, U_FIELD, V_FIELD = 0, 1, 2
SPEED, MASK, P_COLS, V_COLS, U_COLS = range(5)


def iota(shape, axis):
    return lax.broadcasted_iota(jnp.int32, shape, axis)


def split(value, parts):
    pieces = []
    for _ in range(parts):
        piece = value.astype(BF16)
        pieces.append(piece)
        value = value - piece.astype(F32)
    return pieces


def dot(a, b):
    return jnp.dot(a, b, preferred_element_type=F32)


def block_key(index, rows, per_row):
    return (index & (rows - 1)) * per_row + (index >> (rows.bit_length() - 1))


def wide_row(ref):
    return ref[0, 0].reshape(1, ref.shape[-1]).astype(F32)


def upright(row):
    size = row.shape[1]
    diagonal = iota((size, size), 0) == iota((size, size), 1)
    return jnp.sum(jnp.where(diagonal, row, 0.0), axis=1, keepdims=True)


def slot_key(index, blocks, rows, per_row):
    within = block_key(index & (blocks - 1), rows, per_row)
    return ((index >> (blocks.bit_length() - 1)) * blocks + within).astype(F32)


def wide(weights, j):
    return jnp.concatenate([weights[j], weights[j + 1]], axis=1)


def kernel(
    n_gx,
    n_gy,
    state,
    speed_in,
    mask_in,
    vertical_in,
    temp_in,
    coef_in,
    gain_in,
    tile_hbm,
    source_hbm,
    target_hbm,
    weights,
    p2_out,
    u1_out,
    v1_out,
    surface,
    returned,
    speed,
    mask,
    vertical,
    temp,
    coef,
    gain,
    tile_in,
    source_in,
    target_in,
    raw,
    wbuf,
    u0,
    p1,
    u1,
    v1,
    p2,
    p_ext,
    v_ext,
    c_wide,
    w_wide,
    rowsend,
    rowrecv,
    colsend,
    u_recv,
    v_recv,
    p_recv,
    speed_recv,
    mask_recv,
    ybuf,
    yrecv,
    tsend,
    trecv,
    sbuf,
    picked,
    heated,
    load_sem,
    small_sem,
    surface_sem,
    w_sem,
    row_send,
    row_recv,
    col_send,
    col_recv,
    y_send,
    y_recv,
    t_send,
    t_recv,
    out_sem,
):
    sec = lax.axis_index("sec")
    a = lax.axis_index("gx")
    b = lax.axis_index("gy")
    levels, rows, width = state.shape[2:]
    tiles = width // LANES
    pairs, in_width, out_width = wbuf.shape
    in_per_row = width // in_width
    out_per_row = width // out_width
    in_blocks = rows * in_per_row
    out_blocks = rows * out_per_row
    per_chunk = pairs // CHUNKS

    def load(f, i):
        part = state.at[0, f, :, :, pl.ds(i * LANES, LANES)]
        return pltpu.make_async_copy(part, raw.at[f, i], load_sem.at[f, i])

    def load_weights(i):
        part = pl.ds(i * per_chunk, per_chunk)
        return pltpu.make_async_copy(weights.at[0, 0, part], wbuf.at[part], w_sem.at[i])

    small = [
        pltpu.make_async_copy(src, dst, small_sem.at[i])
        for i, (src, dst) in enumerate(
            (
                (speed_in, speed),
                (mask_in, mask),
                (vertical_in, vertical),
                (temp_in, temp),
                (coef_in, coef),
                (gain_in, gain),
                (tile_hbm, tile_in),
                (source_hbm, source_in),
                (target_hbm, target_in),
            )
        )
    ]
    for f in (1, 2):
        for i in range(tiles):
            load(f, i).start()
    for copy in small:
        copy.start()
    for i in range(tiles):
        load(0, i).start()

    @pl.when(sec == 0)
    def _():
        for i in range(CHUNKS):
            load_weights(i).start()

    barrier = pltpu.get_barrier_semaphore()
    for s in range(2):
        for t in range(n_gx):

            @pl.when(jnp.logical_or(s != sec, t != a))
            def _():
                pl.semaphore_signal(barrier, inc=1, device_id=(s, t, b), device_id_type=MESH)

    row_ok = (a > 0, a < n_gx - 1)
    col_ok = (b > 0, b < n_gy - 1)

    for side in range(2):

        @pl.when(col_ok[side])
        def _(side=side):
            pl.semaphore_signal(
                barrier, inc=1, device_id=(sec, a, b + 2 * side - 1), device_id_type=MESH
            )

    beside = (b > 0).astype(jnp.int32) + (b < n_gy - 1).astype(jnp.int32)

    for side in range(2):

        @pl.when(jnp.logical_not(row_ok[side]))
        def _(side=side):
            for buf in (u0, p1, u1, p2):
                buf[side * (rows + 1)] = jnp.zeros(buf.shape[1:], F32)

        @pl.when(jnp.logical_not(col_ok[side]))
        def _(side=side):
            u_recv[side] = jnp.zeros((levels, LANES), F32)
            v_recv[side] = jnp.zeros((levels, LANES), F32)
            p_recv[side] = jnp.zeros((levels, LANES), F32)
            speed_recv[side] = jnp.zeros((rows, LANES), F32)
            mask_recv[side] = jnp.zeros((rows, LANES), jnp.int32)

    def row_copy(exchange, side):
        part = pl.ds(0, 2 * levels if exchange else rowsend.shape[2])
        return pltpu.make_async_remote_copy(
            src_ref=rowsend.at[exchange, side, part],
            dst_ref=rowrecv.at[exchange, 1 - side, part],
            send_sem=row_send.at[exchange, side],
            recv_sem=row_recv.at[exchange, side],
            device_id=(sec, a - 1 if side == 0 else a + 1, b),
            device_id_type=MESH,
        )

    def col_copy(kind, side):
        edge = pl.ds(0 if side == 0 else width - LANES, LANES)
        other = 1 - side
        src, dst = {
            SPEED: (speed.at[0, :, edge], speed_recv.at[other]),
            MASK: (mask.at[0, :, edge], mask_recv.at[other]),
            P_COLS: (colsend.at[P_FIELD, side], p_recv.at[other]),
            V_COLS: (colsend.at[V_FIELD, side], v_recv.at[other]),
            U_COLS: (colsend.at[U_FIELD, side], u_recv.at[other]),
        }[kind]
        return pltpu.make_async_remote_copy(
            src_ref=src,
            dst_ref=dst,
            send_sem=col_send.at[kind, side],
            recv_sem=col_recv.at[kind, side],
            device_id=(sec, a, b - 1 if side == 0 else b + 1),
            device_id_type=MESH,
        )

    def send_cols(*kinds):
        for kind in kinds:
            for side in range(2):

                @pl.when(col_ok[side])
                def _(side=side, kind=kind):
                    col_copy(kind, side).start()

    def wait_cols():
        for kind in range(5):
            for side in range(2):

                @pl.when(col_ok[side])
                def _(side=side, kind=kind):
                    col_copy(kind, 1 - side).wait_recv()

    def wait_sent():
        for side in range(2):
            for kind in range(5):

                @pl.when(col_ok[side])
                def _(side=side, kind=kind):
                    col_copy(kind, side).wait_send()

            for exchange in range(EXCHANGES):

                @pl.when(row_ok[side])
                def _(side=side, exchange=exchange):
                    row_copy(exchange, side).wait_send()

    def send_edges(exchange, u_buf, p_row, v_row):
        for side in range(2):

            @pl.when(row_ok[side])
            def _(side=side):
                x = side * (rows - 1)
                inner = -u_buf[x] if side else u_buf[x + 2]
                c = c_wide[x : x + 1, :]
                partial = p_row(x) - c * (inner + along_y(v_row(x)))
                rowsend[exchange, side, :levels] = u_buf[x + 1].astype(BF16)
                rowsend[exchange, side, levels : 2 * levels] = partial.astype(BF16)
                if exchange == 0:
                    high, low = [piece.astype(F32) for piece in split(c, 2)]
                    at = iota((rowsend.shape[2] - 2 * levels, c.shape[1]), 0)
                    both = jnp.where(at == 0, high, jnp.where(at == 1, low, 0.0))
                    rowsend[exchange, side, 2 * levels :] = both.astype(BF16)
                row_copy(exchange, side).start()

    def wait_edges(exchange, u_buf, p_buf):
        for side in range(2):

            @pl.when(row_ok[side])
            def _(side=side):
                row_copy(exchange, 1 - side).wait_recv()
                at = rows + 1 if side else 0
                u_buf[at] = rowrecv[exchange, side, :levels].astype(F32)
                partial = rowrecv[exchange, side, levels : 2 * levels].astype(F32)
                c = rowrecv[0, side, 2 * levels :].astype(F32)
                term = (c[0:1] + c[1:2]) * u_buf[rows if side else 1]
                p_buf[at] = mix(partial + term if side else partial - term)

    lane = iota((levels, LANES), 1)

    def flat(buf, f):
        return [buf.at[f, i].reshape(levels * rows, LANES) for i in range(tiles)]

    flat_raw = [flat(raw, f) for f in range(3)]

    def column(f, x):
        parts = [ref[pl.ds(x, levels, stride=rows), :] for ref in flat_raw[f]]
        return jnp.concatenate(parts, axis=1)

    def edges(f, x):
        return [flat_raw[f][i][pl.ds(x, levels, stride=rows), :] for i in (0, tiles - 1)]

    def loaded(f):
        for i in range(tiles):
            load(f, i).wait()

    mine = lane // MARGIN

    def pack(f, x, carry):
        low, high = carry
        first, last = edges(f, x)
        low = jnp.where(mine == x, pltpu.roll(first, MARGIN * x, 1), low)
        high = jnp.where(mine == x, pltpu.roll(last, MARGIN * x + MARGIN, 1), high)
        return low, high

    def pack_all(f):
        blank = jnp.zeros((levels, LANES), F32)

        def several(i, carry):
            for k in range(4):
                carry = pack(f, 4 * i + k, carry)
            return carry

        low, high = lax.fori_loop(0, rows // 4, several, (blank, blank))
        colsend[f, 0] = low
        colsend[f, 1] = high

    def margin(ref, x):
        before = pltpu.roll(ref[0], LANES - MARGIN - MARGIN * x, 1)
        after = pltpu.roll(ref[1], lax.rem(LANES - MARGIN * x, LANES), 1)
        rest = jnp.where(lane >= LANES - MARGIN, before, 0.0)
        return jnp.where(lane < MARGIN, after, rest)

    def along_y(value):
        return pltpu.roll(value, value.shape[1] - 1, 1) - pltpu.roll(value, 1, 1)

    def mix(right_side):
        high, low = split(right_side, 2)
        return right_side + dot(mixer, jnp.concatenate([high, low, high, low], axis=0))

    def pressure_row(x, p, u_buf, v):
        divergence = (u_buf[x + 2] - u_buf[x]) + along_y(v)
        return mix(p - c_wide[pl.ds(x, 1), :] * divergence)

    def sweep(row, first, count):
        step = next(k for k in (8, 7, 6, 5, 4, 3, 2, 1) if count % k == 0)

        def several(i, c):
            for k in range(step):
                row(first + i * step + k)
            return c

        lax.fori_loop(0, count // step, several, 0)

    loaded(U_FIELD)
    pack_all(U_FIELD)
    pl.semaphore_wait(barrier, 2 * n_gx - 1 + beside)
    send_cols(U_COLS)
    loaded(V_FIELD)
    pack_all(V_FIELD)
    send_cols(V_COLS)
    for copy in small:
        copy.wait()
    send_cols(SPEED, MASK)
    loaded(P_FIELD)
    pack_all(P_FIELD)
    send_cols(P_COLS)
    m_high, m_low = split(vertical[0], 2)
    m_high, m_low = m_high.astype(F32), m_low.astype(F32)
    mixer = jnp.concatenate([m_high, m_high, m_low, m_low], axis=1).astype(BF16)

    slots = n_gx * out_blocks
    slot_row = wide_row(tile_in) * out_blocks + wide_row(target_in)

    def y_copy(t):
        return pltpu.make_async_remote_copy(
            src_ref=ybuf.at[t],
            dst_ref=yrecv.at[a],
            send_sem=y_send.at[t],
            recv_sem=y_recv.at[a],
            device_id=(1, t, b),
            device_id_type=MESH,
        )

    def t_copy(t):
        return pltpu.make_async_remote_copy(
            src_ref=tsend,
            dst_ref=trecv.at[a],
            send_sem=t_send.at[t],
            recv_sem=t_recv.at[a],
            device_id=(0, t, b),
            device_id_type=MESH,
        )

    def take_fluxes():
        drivers = [
            jnp.concatenate([raw[f, i, 0] for i in range(tiles)], axis=1) for f in range(3)
        ] + [temp[0]]
        heat = jnp.zeros((rows, width), F32)
        factors, gains = coef[...], gain[...]
        for f in range(factors.shape[1]):
            total = factors[0:1, f : f + 1] * drivers[0]
            for k in range(1, 4):
                total = total + factors[k : k + 1, f : f + 1] * drivers[k]
            heat = heat + gains[:, f : f + 1] * jnp.tanh(total).astype(BF16).astype(F32)
        blocks = jnp.concatenate(
            [heat[:, i * in_width : (i + 1) * in_width] for i in range(in_per_row)], axis=0
        )
        source_col = upright(wide_row(source_in))
        key = block_key(iota((pairs, in_blocks), 1), rows, in_per_row).astype(F32)
        picking = (source_col == key).astype(F32).astype(BF16)
        for i, piece in enumerate(split(blocks, 2)):
            picked[i] = dot(picking, piece)

    def regrid(first, last):
        sub = iota((8, out_width), 0)
        for g in range(first, last):
            if g % (per_chunk // 8) == 0:
                load_weights(g * 8 // per_chunk).wait()
            part = slice(8 * g, 8 * g + 8)
            left = jnp.concatenate([picked[0, part], picked[1, part]], axis=0).astype(BF16)
            group = jnp.zeros((8, out_width), F32)
            for i in range(0, 8, 2):
                both = dot(left, wide(wbuf, 8 * g + i))
                both = both[:8] + both[8:]
                group = jnp.where(sub == i, both[:, :out_width], group)
                group = jnp.where(sub == i + 1, both[:, out_width:], group)
            heated[part] = group

    def send_sums():
        placing = (slot_key(iota((slots, pairs), 0), out_blocks, rows, out_per_row) == slot_row).astype(F32).astype(BF16)
        dense = sum(dot(placing, piece) for piece in split(heated[...], 3))
        ybuf[...] = dense.astype(BF16).reshape(n_gx, out_blocks, out_width)
        for t in range(n_gx):
            y_copy(t).start()

    halfway = pairs // 16

    @pl.when(sec == 0)
    def _():
        take_fluxes()
        regrid(0, halfway)

    def fill(x):
        u0[x + 1, :, :width] = column(U_FIELD, x)

    sweep(fill, 0, rows)
    wait_cols()

    def fill_margins(x):
        u0[x + 1, :, width:] = margin(u_recv, x)
        v_ext[x] = margin(v_recv, x)
        p_ext[x] = margin(p_recv, x)

    sweep(fill_margins, 0, rows)
    across = iota((rows, LANES), 1)

    def around(pair):
        rest = jnp.where(across >= LANES - MARGIN, pair[0], 0.0)
        return jnp.where(across < MARGIN, pair[1], rest)

    c_wide[:, :width] = speed[0]
    c_wide[:, width:] = around(speed_recv[...])
    w_wide[:, :width] = mask[0].astype(F32)
    w_wide[:, width:] = around(mask_recv[...].astype(F32))

    def wide_column(f, ext, x):
        return jnp.concatenate([column(f, x), ext[x]], axis=1)

    def p_first(x):
        return wide_column(P_FIELD, p_ext, x)

    def v_first(x):
        return wide_column(V_FIELD, v_ext, x)

    def first_pressure(x):
        p1[x + 1] = pressure_row(x, p_first(x), u0, v_first(x))

    send_edges(0, u0, p_first, v_first)

    @pl.when(sec == 0)
    def _():
        regrid(halfway, pairs // 8)
        send_sums()

    sweep(first_pressure, 1, rows - 2)
    wait_edges(0, u0, p1)
    first_pressure(0)
    first_pressure(rows - 1)

    def first_velocity(x):
        w = w_wide[pl.ds(x, 1), :]
        u1[x + 1] = w * (u0[x + 1] - 0.5 * (p1[x + 2] - p1[x]))
        v1[x] = w * (v_first(x) - 0.5 * along_y(p1[x + 1]))

    for x in (0, 1, rows - 2, rows - 1):
        first_velocity(x)
    send_edges(1, u1, lambda x: p1[x + 1], lambda x: v1[x])
    sweep(first_velocity, 2, rows - 4)

    near = pl.ds(0, width)
    stores = [
        pltpu.make_async_copy(u1.at[pl.ds(1, rows), :, near], u1_out, out_sem.at[0]),
        pltpu.make_async_copy(v1.at[:, :, near], v1_out, out_sem.at[1]),
    ]
    for i, (first, count) in enumerate(((2, rows - 2), (0, 2), (rows, 2))):
        part = pl.ds(first, count)
        stores.append(pltpu.make_async_copy(p2.at[part], p2_out.at[part], out_sem.at[2 + i]))
    stores[0].start()
    stores[1].start()

    def as_blocks(value):
        return jnp.concatenate(
            [value[:, i * out_width : (i + 1) * out_width] for i in range(out_per_row)], axis=0
        )

    @pl.when(sec == 1)
    def _():
        heating = jnp.zeros((out_blocks, out_width), F32)
        for t in range(n_gx):
            pltpu.make_async_remote_copy(
                src_ref=ybuf.at[t],
                dst_ref=yrecv.at[t],
                send_sem=y_send.at[t],
                recv_sem=y_recv.at[t],
                device_id=(0, t, b),
                device_id_type=MESH,
            ).wait_recv()
            heating = heating + yrecv[t].astype(F32)
        ocean = as_blocks(temp[0]) + as_blocks(mask[0].astype(F32)) * heating
        tsend[...] = ocean.astype(BF16)
        for t in range(n_gx):
            t_copy(t).start()

        sbuf[...] = jnp.concatenate(
            [ocean[i * rows : (i + 1) * rows] for i in range(out_per_row)], axis=1
        )
        pltpu.make_async_copy(sbuf, surface.at[0], surface_sem).start()

    def second_pressure(x):
        p2[x + 1] = pressure_row(x, p1[x + 1], u1, v1[x])

    sweep(second_pressure, 1, rows - 2)
    stores[2].start()
    wait_edges(1, u1, p2)
    second_pressure(0)
    second_pressure(rows - 1)
    stores[3].start()
    stores[4].start()

    @pl.when(sec == 0)
    def _():
        for t in range(n_gx):
            pltpu.make_async_remote_copy(
                src_ref=tsend,
                dst_ref=trecv.at[t],
                send_sem=t_send.at[t],
                recv_sem=t_recv.at[t],
                device_id=(1, t, b),
                device_id_type=MESH,
            ).wait_recv()
        pltpu.make_async_copy(trecv, returned, surface_sem).start()

    wait_sent()

    @pl.when(sec == 0)
    def _():
        for t in range(n_gx):
            y_copy(t).wait_send()
        pltpu.make_async_copy(trecv, returned, surface_sem).wait()

    @pl.when(sec == 1)
    def _():
        for t in range(n_gx):
            t_copy(t).wait_send()
        pltpu.make_async_copy(sbuf, surface.at[0], surface_sem).wait()

    for copy in stores:
        copy.wait()


def last_kernel(
    p_in,
    u_in,
    v_in,
    mask_in,
    surface_in,
    returned_in,
    tile_hbm,
    source_hbm,
    target_hbm,
    weights,
    final,
    surface,
    p,
    u,
    v,
    mask,
    returned,
    tile_in,
    source_in,
    target_in,
    wbuf,
    sbuf,
    out,
    sem,
    out_sem,
    small_sem,
    w_sem,
):
    sec = lax.axis_index("sec")
    rows, levels, width = u_in.shape
    tiles = width // LANES
    parts = rows // 4
    half = 8

    mask_copy = pltpu.make_async_copy(mask_in, mask, small_sem.at[0])
    mask_copy.start()
    loads = []
    for k in range(parts):
        first = 0 if k == 0 else 4 * k + 2
        p_rows = pl.ds(first, 4 * k + 6 - first)
        part = pl.ds(4 * k, 4)
        loads.append(
            [
                pltpu.make_async_copy(src, dst, sem.at[k, i])
                for i, (src, dst) in enumerate(
                    (
                        (p_in.at[p_rows], p.at[p_rows]),
                        (u_in.at[part], u.at[part]),
                        (v_in.at[part], v.at[part]),
                    )
                )
            ]
        )
        for copy in loads[-1]:
            copy.start()
    small = [
        pltpu.make_async_copy(src, dst, small_sem.at[2 + i])
        for i, (src, dst) in enumerate(
            (
                (returned_in, returned),
                (tile_hbm, tile_in),
                (source_hbm, source_in),
                (target_hbm, target_in),
            )
        )
    ]
    pairs, in_width, out_width = wbuf.shape
    per_chunk = pairs // CHUNKS

    def load_weights(i):
        group = pl.ds(i * per_chunk, per_chunk)
        return pltpu.make_async_copy(weights.at[0, 0, group], wbuf.at[group], w_sem.at[i])

    @pl.when(sec == 0)
    def _():
        for copy in small:
            copy.start()
        for i in range(CHUNKS):
            load_weights(i).start()

    @pl.when(sec == 1)
    def _():
        pltpu.make_async_copy(surface_in, surface, small_sem.at[1]).start()

    mask_copy.wait()

    def store(h, f, i):
        part = final.at[0, f, :, pl.ds(h * half, half), pl.ds(i * LANES, LANES)]
        return pltpu.make_async_copy(out.at[h, f, i], part, out_sem.at[h, f, i])

    stores = [store(h, f, i) for h in range(rows // half) for f in range(3) for i in range(tiles)]
    for k in range(parts):
        for copy in loads[k]:
            copy.wait()
        for x in range(4 * k, 4 * k + 4):
            h = x // half
            w = mask[0, x : x + 1, :].astype(F32)
            here = p[x + 1]
            span = here.shape[1]
            plus = pltpu.roll(here, span - 1, 1)[:, :width]
            minus = pltpu.roll(here, 1, 1)[:, :width]
            gradient = p[x + 2, :, :width] - p[x, :, :width]
            values = (
                here[:, :width],
                w * (u[x] - 0.5 * gradient),
                w * (v[x] - 0.5 * (plus - minus)),
            )
            for f, value in enumerate(values):
                for i in range(tiles):
                    flat = out.at[h, f, i].reshape(levels * half, LANES)
                    at = pl.ds(x % half, levels, stride=half)
                    flat[at, :] = value[:, i * LANES : (i + 1) * LANES]
        if (4 * k + 4) % half == 0:
            per_half = 3 * tiles
            h = (4 * k + 4) // half - 1
            for copy in stores[h * per_half : (h + 1) * per_half]:
                copy.start()

    @pl.when(sec == 0)
    def _():
        for copy in small:
            copy.wait()
        in_per_row, out_per_row = width // in_width, width // out_width
        in_blocks, out_blocks = rows * in_per_row, rows * out_per_row
        slots = returned.shape[0] * out_blocks
        slot_col = upright(wide_row(tile_in) * out_blocks + wide_row(target_in))
        slot = slot_key(iota((pairs, slots), 1), out_blocks, rows, out_per_row)
        picking = (slot == slot_col).astype(F32).astype(BF16)
        per_pair = dot(picking, returned[...].reshape(slots, out_width))
        key = block_key(iota((in_blocks, pairs), 0), rows, in_per_row).astype(F32)
        owner = (key == wide_row(source_in)).astype(F32)
        total = jnp.zeros((in_blocks, in_width), F32)
        for j in range(0, pairs, 2):
            if j % per_chunk == 0:
                load_weights(j // per_chunk).wait()
            left = jnp.concatenate(
                [owner[:, i : i + 1] * per_pair[i : i + 1] for i in (j, j + 1)], axis=1
            ).astype(BF16)
            total = total + lax.dot_general(
                left, wide(wbuf, j), (((1,), (1,)), ((), ())), preferred_element_type=F32
            )
        sbuf[...] = jnp.concatenate(
            [total[i * rows : (i + 1) * rows] for i in range(in_per_row)], axis=1
        )
        surface_copy = pltpu.make_async_copy(sbuf, surface.at[0], small_sem.at[1])
        surface_copy.start()
        surface_copy.wait()

    @pl.when(sec == 1)
    def _():
        pltpu.make_async_copy(surface_in, surface, small_sem.at[1]).wait()

    for copy in stores:
        copy.wait()


def local(n_gx, n_gy, *args):
    state, speed, mask, vertical, temp, coef, gain, tile, source, target, weights = args
    coef = coef.T
    gain = gain.reshape(1, -1)
    tile = tile.reshape(source.shape)
    _, fields, levels, rows, width = state.shape
    pairs, in_width, out_width = weights.shape[2:]
    out_blocks = rows * width // out_width
    hbm = pl.BlockSpec(memory_space=pltpu.HBM)
    free = pl.BlockSpec(memory_space=pl.ANY)
    dma = pltpu.SemaphoreType.DMA
    tiled = pltpu.VMEM((fields, width // LANES, levels, rows, LANES), F32)
    span = width + LANES
    tall = pltpu.VMEM((rows + 2, levels, span), F32)
    ext = pltpu.VMEM((rows, levels, LANES), F32)
    params = dict(has_side_effects=True, vmem_limit_bytes=62 * 2**20)
    p2, u1, v1, surface, returned = pl.pallas_call(
        functools.partial(kernel, n_gx, n_gy),
        out_shape=(
            jax.ShapeDtypeStruct((rows + 2, levels, span), F32),
            jax.ShapeDtypeStruct((rows, levels, width), F32),
            jax.ShapeDtypeStruct((rows, levels, width), F32),
            jax.ShapeDtypeStruct(temp.shape, F32),
            jax.ShapeDtypeStruct((n_gx, out_blocks, out_width), BF16),
        ),
        in_specs=[hbm] * 11,
        out_specs=(free,) * 5,
        scratch_shapes=[
            pltpu.VMEM(speed.shape, F32),
            pltpu.VMEM(mask.shape, jnp.int32),
            pltpu.VMEM(vertical.shape, F32),
            pltpu.VMEM(temp.shape, F32),
            pltpu.VMEM(coef.shape, F32),
            pltpu.VMEM(gain.shape, F32),
            pltpu.VMEM(tile.shape, jnp.int32),
            pltpu.VMEM(source.shape, jnp.int32),
            pltpu.VMEM(target.shape, jnp.int32),
            tiled,
            pltpu.VMEM((pairs, in_width, out_width), BF16),
            tall,
            tall,
            tall,
            pltpu.VMEM((rows, levels, span), F32),
            tall,
            ext,
            ext,
            pltpu.VMEM((rows, span), F32),
            pltpu.VMEM((rows, span), F32),
            pltpu.VMEM((EXCHANGES, 2, 2 * levels + 16, span), BF16),
            pltpu.VMEM((EXCHANGES, 2, 2 * levels + 16, span), BF16),
            pltpu.VMEM((fields, 2, levels, LANES), F32),
            pltpu.VMEM((2, levels, LANES), F32),
            pltpu.VMEM((2, levels, LANES), F32),
            pltpu.VMEM((2, levels, LANES), F32),
            pltpu.VMEM((2, rows, LANES), F32),
            pltpu.VMEM((2, rows, LANES), jnp.int32),
            pltpu.VMEM((n_gx, out_blocks, out_width), BF16),
            pltpu.VMEM((n_gx, out_blocks, out_width), BF16),
            pltpu.VMEM((out_blocks, out_width), BF16),
            pltpu.VMEM((n_gx, out_blocks, out_width), BF16),
            pltpu.VMEM((rows, width), F32),
            pltpu.VMEM((2, pairs, in_width), F32),
            pltpu.VMEM((pairs, out_width), F32),
            dma((fields, width // LANES)),
            dma((9,)),
            dma(()),
            dma((CHUNKS,)),
            dma((EXCHANGES, 2)),
            dma((EXCHANGES, 2)),
            dma((5, 2)),
            dma((5, 2)),
            dma((n_gx,)),
            dma((n_gx,)),
            dma((n_gx,)),
            dma((n_gx,)),
            dma((5,)),
        ],
        compiler_params=pltpu.CompilerParams(collective_id=0, **params),
    )(state, speed, mask, vertical, temp, coef, gain, tile, source, target, weights)
    return pl.pallas_call(
        last_kernel,
        out_shape=(
            jax.ShapeDtypeStruct(state.shape, F32),
            jax.ShapeDtypeStruct(temp.shape, F32),
        ),
        in_specs=[hbm] * 10,
        out_specs=(free, free),
        scratch_shapes=[
            tall,
            pltpu.VMEM((rows, levels, width), F32),
            pltpu.VMEM((rows, levels, width), F32),
            pltpu.VMEM(mask.shape, jnp.int32),
            pltpu.VMEM(returned.shape, BF16),
            pltpu.VMEM(tile.shape, jnp.int32),
            pltpu.VMEM(source.shape, jnp.int32),
            pltpu.VMEM(target.shape, jnp.int32),
            pltpu.VMEM((pairs, in_width, out_width), BF16),
            pltpu.VMEM((rows, width), F32),
            pltpu.VMEM((rows // 8, fields, width // LANES, levels, 8, LANES), F32),
            dma((rows // 4, 3)),
            dma((rows // 8, fields, width // LANES)),
            dma((6,)),
            dma((CHUNKS,)),
        ],
        compiler_params=pltpu.CompilerParams(**params),
    )(p2, u1, v1, mask, surface, returned, tile, source, target, weights)


def solution(mesh):
    return jax.shard_map(
        functools.partial(local, mesh.shape["gx"], mesh.shape["gy"]),
        mesh=mesh,
        in_specs=(
            P("sec", None, None, "gx", "gy"),
            P("sec", "gx", "gy"),
            P("sec", "gx", "gy"),
            P("sec", None, None),
            P("sec", "gx", "gy"),
            P(),
            P(),
            P("gx", "gy", None, None),
            P("gx", "gy", None),
            P("gx", "gy", None),
            P("gx", "gy", None, None, None),
        ),
        out_specs=(P("sec", None, None, "gx", "gy"), P("sec", "gx", "gy")),
        check_vma=False,
    )
```
